512 devices in a mesh: row: 32 (over z, core), col: 16 (over x, y).
Axes of the slice: x: 4, y: 4, z: 16, core: 2. Of those that a mesh axis runs over, the one named last changes fastest.
Arguments:
- boxes: int32 [4, 2097152], P(None, ('row', 'col')), may hold values from 0 to 4095, as said below
- pins: int32 [2097152], P(('row', 'col')), may hold values from 2 to 32
- cell_bins: int32 [2, 8388608], P(None, ('row', 'col')), may hold values from 0 to 4095, as said below
- cell_area: int32 [8388608], P(('row', 'col')), may hold values from 1 to 64
Outputs:
- demand: float32 [4096, 4096], P('row', 'col')
- density: float32 [4096, 4096], P('row', 'col')
The draws below stay inside these ranges and needn't reach their ends.
Inputs may be any that keep to these rules, and one draw needn't show every extreme that they name: `boxes`: nets are in blocks of 4096, one block per device in the order of the row+col index; the lower corner (y0, x0) of a net lies in that device's 128 x 256 bins. y0 <= y1 < 4096, x0 <= x1 < 4096, y1 - y0 + 1 <= 64 and x1 - x0 + 1 <= 128. `cell_bins`: cells are in blocks of 16384, one block per device in the order of the row+col index; each cell's bin lies in that device's bins.
All inputs are finite; a program needn't handle non-finite values.
Results may differ from the reference program's by a relative error of at most 0.0025.
Values sent between devices are 32-bit elements; how exact they have to be, the bound alone decides.
No kernel may reach another device: no remote copies, remote signals or barrier semaphores. Data moves between devices by JAX's collectives and lax.ppermute only.
A program may use at most 64 MiB of HBM per device.

```python
import jax
import jax.numpy as jnp

BR = 128
BC = 256
NETS_DEV = 4096
CELLS_DEV = 16384
STEPS = 6
NY = 4096
NX = 4096
NETS = 2097152
CELLS = 8388608


def draw_boxes(key, part):
    keys = jax.random.split(jax.random.fold_in(key, 11), 6)
    owner = jnp.arange(NETS, dtype=jnp.int32) // NETS_DEV
    bands = NX // BC
    band_row = owner // bands
    band_col = owner % bands
    y_lo = band_row * BR + jax.random.randint(keys[0], (NETS,), 0, BR)
    x_lo = band_col * BC + jax.random.randint(keys[1], (NETS,), 0, BC)
    level_y = jax.random.randint(keys[2], (NETS,), 0, BR.bit_length() - 1)
    level_x = jax.random.randint(keys[3], (NETS,), 0, BC.bit_length() - 1)
    height = jax.random.randint(keys[4], (NETS,), 1, jnp.left_shift(1, level_y) + 1)
    width = jax.random.randint(keys[5], (NETS,), 1, jnp.left_shift(1, level_x) + 1)
    y_hi = jnp.minimum(y_lo + height - 1, NY - 1)
    x_hi = jnp.minimum(x_lo + width - 1, NX - 1)
    return jnp.stack([y_lo, y_hi, x_lo, x_hi]).astype(jnp.int32)


def draw_cell_bins(key, part):
    keys = jax.random.split(jax.random.fold_in(key, 23), 2)
    owner = jnp.arange(CELLS, dtype=jnp.int32) // CELLS_DEV
    bands = NX // BC
    rows = owner // bands * BR + jax.random.randint(keys[0], (CELLS,), 0, BR)
    cols = owner % bands * BC + jax.random.randint(keys[1], (CELLS,), 0, BC)
    return jnp.stack([rows, cols]).astype(jnp.int32)


def set_ends(values, stream_key, least, high):
    dims = values.shape
    index_at = [jax.random.randint(jax.random.fold_in(stream_key, axis), (), 0, dims[axis]) for axis in range(len(dims))]
    values = values.at[tuple(index_at)].set(least)
    longest = dims.index(max(dims))
    index_at[longest] = (index_at[longest] + 1) % dims[longest]
    return values.at[tuple(index_at)].set(high)


def setup_inputs(seed: int = 0) -> dict:
    key_list = jax.random.split(jax.random.key(seed), 5)
    return {
        "boxes": draw_boxes(jax.random.fold_in(key_list[4], 71), 0),
        "pins": set_ends(jax.random.randint(key_list[1], (NETS,), 2, 33), jax.random.fold_in(key_list[1], 1), 2, 32).astype(jnp.int32),
        "cell_bins": draw_cell_bins(jax.random.fold_in(key_list[4], 71), 0),
        "cell_area": set_ends(jax.random.randint(key_list[3], (CELLS,), 1, 65), jax.random.fold_in(key_list[3], 1), 1, 64).astype(jnp.int32),
    }


def reference(boxes, pins, cell_bins, cell_area):
    y_lo, y_hi, x_lo, x_hi = boxes[0], boxes[1], boxes[2], boxes[3]
    width = (x_hi - x_lo + 1).astype(jnp.float32)
    height = (y_hi - y_lo + 1).astype(jnp.float32)
    weight = pins.astype(jnp.float32) * (width + height) / (width * height) / 16.0
    impulse = jnp.zeros((NY, NX), jnp.float32)
    impulse = impulse.at[y_lo, x_lo].add(weight, mode="drop")
    impulse = impulse.at[y_lo, x_hi + 1].add(-weight, mode="drop")
    impulse = impulse.at[y_hi + 1, x_lo].add(-weight, mode="drop")
    impulse = impulse.at[y_hi + 1, x_hi + 1].add(weight, mode="drop")
    across = jnp.cumsum(impulse, axis=1)
    demand = jnp.cumsum(across, axis=0)
    area_sum = jnp.zeros((NY, NX), jnp.float32).at[cell_bins[0], cell_bins[1]].add(cell_area.astype(jnp.float32))
    density = (1.0 + 1.5 * demand / (1.0 + demand)) * area_sum / 16.0
    for step in range(STEPS):
        padded = jnp.pad(density, 1)
        beside = padded[2:, 1:-1] + padded[:-2, 1:-1] + padded[1:-1, 2:] + padded[1:-1, :-2]
        density = density + 0.24 * (beside - 4.0 * density)
    return demand, density
```

```python
import jax
import jax.numpy as jnp
from jax import lax
from jax.experimental import pallas as pl
from jax.experimental.pallas import tpu as pltpu
from jax.sharding import PartitionSpec as P

BR = 128
BC = 256
STEPS = 6
TALL = 192
WIDE = 384
NET_BLOCK = 512
CELL_BLOCK = 1024
VMEM = pltpu.MemorySpace.VMEM


def rows_of(value, rows):
    return jnp.broadcast_to(value.astype(jnp.float32), (16, value.shape[1])).astype(jnp.bfloat16)[None]


def steps_of(rows, shift, n):
    base = lax.broadcasted_iota(jnp.int32, (rows // 16, 16, n), 0) * 16
    base = base + lax.broadcasted_iota(jnp.int32, (rows // 16, 16, n), 1) - shift
    return base.astype(jnp.float32).astype(jnp.bfloat16)


def lane_row(ref, first, n):
    return jnp.concatenate([ref[pl.ds(first // 128 + i, 1), :] for i in range(n // 128)], axis=1)


def nt_dot(left, right):
    return lax.dot_general(
        left, right, (((1,), (1,)), ((), ())), preferred_element_type=jnp.float32
    )


def window_kernel(place, boxes, pins, bins, area, d_out, a_out, right_out, left_out):
    row_first = place[0] * BR
    col_first = place[1] * BC
    zero = jnp.zeros((), jnp.bfloat16)
    one = jnp.ones((), jnp.bfloat16)
    n = NET_BLOCK
    demand = jnp.zeros((TALL, WIDE), jnp.float32)
    for k in range(4096 // n):
        box = boxes[:, k * n : (k + 1) * n]
        y0, y1, x0, x1 = (box[i : i + 1] for i in range(4))
        w = (x1 - x0 + 1).astype(jnp.float32)
        h = (y1 - y0 + 1).astype(jnp.float32)
        weight = lane_row(pins, k * n, n).astype(jnp.float32) * (w + h) / (w * h) / 16.0
        high = weight.astype(jnp.bfloat16)
        low = (weight - high.astype(jnp.float32)).astype(jnp.bfloat16)
        high = rows_of(high, 16)
        low = rows_of(low, 16)
        rows = steps_of(TALL, 0, n)
        inside = (rows >= rows_of(y0 - row_first, 16)) & (rows <= rows_of(y1 - row_first, 16))
        left = jnp.where(inside, one, zero).reshape(TALL, n)
        cols = steps_of(WIDE, 192, n)
        x0 = rows_of(x0 - (col_first + 192), 16)
        x1 = rows_of(x1 - (col_first + 192), 16)
        inside = (cols >= x0) & (cols <= x1)
        demand = demand + nt_dot(left, jnp.where(inside, high, zero).reshape(WIDE, n))
        demand = demand + nt_dot(left, jnp.where(inside, low, zero).reshape(WIDE, n))
    n = CELL_BLOCK
    total = jnp.zeros((BR, BC), jnp.float32)
    for k in range(16384 // n):
        where = bins[:, k * n : (k + 1) * n]
        left = steps_of(BR, 0, n) == rows_of(where[0:1] - row_first, 16)
        left = jnp.where(left, one, zero).reshape(BR, n)
        right = steps_of(BC, 0, n) == rows_of(where[1:2] - col_first, 16)
        right = jnp.where(right, rows_of(lane_row(area, k * n, n), 16), zero).reshape(BC, n)
        total = total + nt_dot(left, right)
    total = total * (1.0 / 16.0)
    d_out[...] = demand[:, :BC]
    a_out[...] = total
    right_out[:TALL] = demand[:, BC:]
    pad = jnp.zeros((64, 128), jnp.float32)
    edge = jnp.concatenate([demand[:, 128:BC], pad], axis=0).T[120:128]
    right_out[TALL : TALL + 8] = edge[:, :128]
    right_out[TALL + 8 : TALL + 16] = edge[:, 128:]
    right_out[TALL + 16 : TALL + 24] = total[:, 128:].T[120:128]
    edge = jnp.concatenate([demand[:, :128], pad], axis=0).T[:8]
    left_out[:8] = edge[:, :128]
    left_out[8:16] = edge[:, 128:]
    left_out[16:24] = total[:, :128].T[:8]


def stand(strip, at):
    length = strip.shape[1]
    parts = [strip]
    if at:
        parts = [jnp.zeros((at, length), jnp.float32)] + parts
    if at < 120:
        parts = parts + [jnp.zeros((120 - at, length), jnp.float32)]
    return jnp.concatenate(parts, axis=0).T


def merge_kernel(d_in, a_in, over, from_left, from_right, d_out, a_out, down_out, up_out):
    low = d_in[:, :128] + from_left[:TALL]
    mid = d_in[:, 128:]
    edge = jnp.concatenate([from_left[TALL : TALL + 8], from_left[TALL + 8 : TALL + 16]], axis=1)
    edge = stand(edge, 120)[:TALL]
    after = jnp.concatenate([from_right[:8], from_right[8:16]], axis=1)
    after = stand(after, 0)[:TALL]
    lane = lax.broadcasted_iota(jnp.int32, (TALL, 128), 1)
    high = jnp.where(lane < 6, over[:TALL] + after, jnp.where(lane >= 122, edge, 0.0))
    a_edge = stand(from_left[TALL + 16 :], 120)
    a_after = stand(from_right[16:], 0)
    lane = lane[:BR]
    a_high = jnp.where(lane < 6, a_after, jnp.where(lane >= 122, a_edge, 0.0))
    d_out[:, :128] = low[:BR]
    d_out[:, 128:256] = mid[:BR]
    d_out[:, 256:] = high[:BR]
    a_out[:, :256] = a_in[...]
    a_out[:, 256:] = a_high
    for i, block in enumerate((low, mid, high)):
        lanes = slice(128 * i, 128 * (i + 1))
        down_out[:64, lanes] = block[128:]
        down_out[64:72, lanes] = block[120:128]
        up_out[:8, lanes] = block[:8]
    down_out[72:80, :256] = a_in[120:128]
    down_out[72:80, 256:] = a_high[120:128]
    up_out[8:, :256] = a_in[:8]
    up_out[8:, 256:] = a_high[:8]


def final_kernel(place, d_in, a_in, over, from_above, from_below, demand_out, density_out):
    top = from_above[64:72]
    own = jnp.concatenate([d_in[:64] + from_above[:64], d_in[64:]], axis=0)
    bottom = over[...] + from_below[:8]
    demand_out[...] = own[:, :BC]
    demand = jnp.concatenate([top, own, bottom], axis=0)
    area = jnp.concatenate([from_above[72:80], a_in[...], from_below[8:]], axis=0)
    shape = demand.shape
    row = lax.broadcasted_iota(jnp.int32, shape, 0) - 8 + place[0] * BR
    lane = lax.broadcasted_iota(jnp.int32, shape, 1)
    col = jnp.where(lane < 320, lane, lane - WIDE)
    near = (col >= -6) & (col < BC + 6)
    col = col + place[1] * BC
    inside = near & (row >= 0) & (row < place[2]) & (col >= 0) & (col < place[3])
    start = (1.0 + 1.5 * demand / (1.0 + demand)) * area
    density = jnp.where(inside, start, 0.0)
    keep = jnp.where(inside, 0.04, 0.0)
    gain = jnp.where(inside, 0.24, 0.0)
    for _ in range(STEPS):
        beside = (
            pltpu.roll(density, 1, 0)
            + pltpu.roll(density, shape[0] - 1, 0)
            + pltpu.roll(density, 1, 1)
            + pltpu.roll(density, shape[1] - 1, 1)
        )
        density = keep * density + gain * beside
    density_out[...] = density[8 : 8 + BR, :BC]


def shift(block, axis, distance):
    devices = range(lax.axis_size(axis))
    route = [(i, i + distance) for i in devices if i + distance in devices]
    return lax.ppermute(block, axis, route)


def call(kernel, shapes, *args, scalars=0):
    specs = [pl.BlockSpec(memory_space=pltpu.MemorySpace.SMEM)] * scalars
    specs = specs + [pl.BlockSpec(memory_space=VMEM)] * (len(args) - scalars)
    return pl.pallas_call(
        kernel,
        out_shape=[jax.ShapeDtypeStruct(s, jnp.float32) for s in shapes],
        in_specs=specs,
        out_specs=[pl.BlockSpec(memory_space=VMEM)] * len(shapes),
        compiler_params=pltpu.CompilerParams(vmem_limit_bytes=48 * 2**20),
    )(*args)


def body(boxes, pins, cell_bins, cell_area):
    place = jnp.stack(
        [
            lax.axis_index("row"),
            lax.axis_index("col"),
            lax.axis_size("row") * BR,
            lax.axis_size("col") * BC,
        ]
    ).astype(jnp.int32)
    d_own, a_own, right, left = call(
        window_kernel,
        [(TALL, BC), (BR, BC), (TALL + 24, 128), (24, 128)],
        place,
        boxes,
        pins.reshape(-1, 128),
        cell_bins,
        cell_area.reshape(-1, 128),
        scalars=1,
    )
    from_left = shift(right, "col", 1)
    from_right = shift(left, "col", -1)
    d_ext, a_ext, down, up = call(
        merge_kernel,
        [(BR, WIDE), (BR, WIDE), (80, WIDE), (16, WIDE)],
        d_own,
        a_own,
        right,
        from_left,
        from_right,
    )
    from_above = shift(down, "row", 1)
    from_below = shift(up, "row", -1)
    demand, density = call(
        final_kernel,
        [(BR, BC), (BR, BC)],
        place,
        d_ext,
        a_ext,
        down[:8],
        from_above,
        from_below,
        scalars=1,
    )
    return (demand, density)


def solution(mesh):
    return jax.shard_map(
        body,
        mesh=mesh,
        in_specs=(
            P(None, ("row", "col")),
            P(("row", "col")),
            P(None, ("row", "col")),
            P(("row", "col")),
        ),
        out_specs=(P("row", "col"), P("row", "col")),
        check_vma=False,
    )
```

```python
import jax
import jax.numpy as jnp
from jax import lax
from jax.experimental import pallas as pl
from jax.experimental.pallas import tpu as pltpu
from jax.sharding import PartitionSpec as P

BR = 128
BC = 256
STEPS = 6
TALL = 192
WIDE = 384
NET_BLOCK = 1024
CELL_BLOCK = 1024
FACTORS = 24
F32 = jnp.float32
BF16 = jnp.bfloat16
FP8 = jnp.float8_e4m3fn
VMEM = pltpu.MemorySpace.VMEM
HBM = pltpu.MemorySpace.HBM


def repeated(value, rows, dtype):
    if dtype != jnp.int8:
        value = value.astype(F32)
    return jnp.broadcast_to(value, (rows, value.shape[1])).astype(dtype)[None]


def ruler(length, rows, shift, n, dtype):
    shape = (length // rows, rows, n)
    place = lax.broadcasted_iota(jnp.int32, shape, 0) * rows
    place = place + lax.broadcasted_iota(jnp.int32, shape, 1) - shift
    return place.astype(dtype) if dtype == jnp.int8 else place.astype(F32).astype(dtype)


def lane_row(ref, first, n):
    return jnp.concatenate([ref[pl.ds(first // 128 + i, 1), :] for i in range(n // 128)], axis=1)


def nt_dot(left, right):
    return lax.dot_general(left, right, (((1,), (1,)), ((), ())), preferred_element_type=F32)


def split_weights(boxes, pins, row_factor, col_factor):
    width = boxes[3:4, :] - boxes[2:3, :] + 1
    height = boxes[1:2, :] - boxes[0:1, :] + 1
    nets = width.shape[1]
    width, height = (
        jnp.concatenate([v[:, i : i + 128] for i in range(0, nets, 128)], axis=0).astype(F32)
        for v in (width, height)
    )
    weight = pins[...].astype(F32) * (width + height) / (width * height) * (1.0 / 16.0)
    best = weight
    for k in range(FACTORS):
        one = 1.0 + k / 128.0
        other = (weight * (1.0 / one)).astype(BF16).astype(F32)
        error = jnp.abs(other * one - weight)
        if k == 0:
            best, row_part, col_part = error, jnp.ones_like(weight), other
        else:
            better = error < best
            best = jnp.where(better, error, best)
            row_part = jnp.where(better, one, row_part)
            col_part = jnp.where(better, other, col_part)
    row_factor[...] = row_part
    col_factor[...] = col_part


def window_kernel(
    boxes_in, pins_in, bins_in, area_in, d_out, a_out, even_out, odd_out,
    boxes, pins, bins, area, row_factor, col_factor, sems,
):
    copies = [
        pltpu.make_async_copy(source, target, sems.at[i])
        for i, (source, target) in enumerate(
            ((boxes_in, boxes), (pins_in, pins), (bins_in, bins), (area_in, area))
        )
    ]
    for copy in copies:
        copy.start()
    copies[0].wait()
    copies[1].wait()
    split_weights(boxes, pins, row_factor, col_factor)
    n = NET_BLOCK
    zero = jnp.zeros((), BF16)
    demand = jnp.zeros((WIDE, TALL), F32)
    for k in range(0, boxes.shape[1], n):
        box = boxes[:, k : k + n]
        y0, y1, x0, x1 = (box[i : i + 1] for i in range(4))
        top = y0 & (BR - 1)
        bottom = y1 - (y0 - top)
        start = x0 & (BC - 1)
        end = x1 - (x0 - start)
        rows = ruler(TALL, 16, 0, n, BF16)
        inside = (rows >= repeated(top, 16, BF16)) & (rows <= repeated(bottom, 16, BF16))
        down = jnp.where(inside, repeated(lane_row(row_factor, k, n), 16, BF16), zero)
        cols = ruler(WIDE, 16, 192, n, BF16)
        inside = (cols >= repeated(start - 192, 16, BF16)) & (
            cols <= repeated(end - 192, 16, BF16)
        )
        right = jnp.where(inside, repeated(lane_row(col_factor, k, n), 16, BF16), zero)
        demand = demand + nt_dot(right.reshape(WIDE, n), down.reshape(TALL, n))
    copies[2].wait()
    copies[3].wait()
    n = CELL_BLOCK
    zero = jnp.zeros((), FP8)
    one = jnp.ones((), FP8)
    total = jnp.zeros((BC, 2 * BR), F32)
    for k in range(0, bins.shape[1], n):
        where = bins[:, k : k + n]
        size = lane_row(area, k, n)
        rows = ruler(BR, 32, 0, n, jnp.int8) == repeated(where[0:1] & (BR - 1), 32, jnp.int8)
        down = jnp.concatenate(
            [
                jnp.where(rows, repeated(part, 32, FP8), zero).reshape(BR, n)
                for part in (size >> 3, size & 7)
            ],
            axis=0,
        )
        cols = ruler(BC, 32, 128, n, jnp.int8) == repeated(
            (where[1:2] & (BC - 1)) - 128, 32, jnp.int8
        )
        right = jnp.where(cols, one, zero).reshape(BC, n)
        total = total + nt_dot(right, down)
    demand = demand.T
    total = (total[:, :BR] * 0.5 + total[:, BR:] * (1.0 / 16.0)).T
    d_out[...] = demand[: BR + 8]
    a_out[...] = total
    even = lax.rem(lax.axis_index("row"), 2) == 0
    for message, goes_down in ((even_out, even), (odd_out, jnp.logical_not(even))):
        message[:8] = jnp.where(goes_down, demand[BR : BR + 8], demand[:8])
        message[8:64] = demand[BR + 8 :]
        message[64:72] = demand[BR - 8 : BR]
        message[72:, :BC] = jnp.where(goes_down, total[BR - 8 :], total[:8])


def merge_kernel(d_own, a_own, even_in, odd_in, d_out, a_out, even_out, odd_out):
    even = lax.rem(lax.axis_index("row"), 2) == 0
    above = jnp.where(even, odd_in[...], even_in[...])
    below = jnp.where(even, even_in[:8], odd_in[:8])
    below_area = jnp.where(even, even_in[72:, :BC], odd_in[72:, :BC])
    demand = jnp.concatenate(
        [d_own[:64] + above[:64], d_own[64:BR], d_own[BR:] + below, above[64:72]], axis=0
    )
    area = jnp.concatenate([a_own[...], below_area, above[72:, :BC]], axis=0)
    d_out[...] = demand
    a_out[...] = area
    lane = lax.broadcasted_iota(jnp.int32, (BR + 16, 128), 1)
    leftward = jnp.where(lane < 8, demand[:, :128], pltpu.roll(area[:, :128], 8, 1))
    strip = jnp.where(lane < 120, pltpu.roll(demand[:, 128:BC], 120, 1), area[:, 128:])
    strip = jnp.concatenate([strip, jnp.zeros((112, 128), F32)], axis=0).T[112:]
    even = lax.rem(lax.axis_index("col"), 2) == 0
    for message, goes_right in ((even_out, even), (odd_out, jnp.logical_not(even))):
        message[: BR + 16] = jnp.where(goes_right, demand[:, BC:], leftward)
        message[BR + 16 : BR + 32] = strip[:, :128]
        message[BR + 32 :] = strip[:, 128:]


def final_kernel(d_in, a_in, even_in, odd_in, demand_out, density_out):
    tall = BR + 16
    even = lax.rem(lax.axis_index("col"), 2) == 0
    left = jnp.where(even, odd_in[...], even_in[...])
    right = jnp.where(even, even_in[:tall], odd_in[:tall])
    strip = jnp.concatenate([left[tall : tall + 16], left[tall + 16 :]], axis=1)
    strip = jnp.concatenate([jnp.zeros((112, 256), F32), strip], axis=0).T[:tall]
    lane = lax.broadcasted_iota(jnp.int32, (tall, 128), 1)
    beyond = jnp.where(lane < 8, d_in[:, BC:] + right, pltpu.roll(strip, 8, 1))
    demand = jnp.concatenate([d_in[:, :128] + left[:tall], d_in[:, 128:BC], beyond], axis=1)
    beyond = jnp.where(lane < 8, pltpu.roll(right, 120, 1), strip)
    area = jnp.concatenate([a_in[...], beyond], axis=1)
    demand_out[...] = demand[:BR, :BC]
    shape = demand.shape
    row = lax.broadcasted_iota(jnp.int32, shape, 0)
    row = jnp.where(row < BR + 8, row, row - tall) + lax.axis_index("row") * BR
    lane = lax.broadcasted_iota(jnp.int32, shape, 1)
    near = (lane < BC + 8) | (lane >= WIDE - 8)
    col = jnp.where(lane < BC + 8, lane, lane - WIDE) + lax.axis_index("col") * BC
    rows, cols = lax.axis_size("row") * BR, lax.axis_size("col") * BC
    inside = near & (row >= 0) & (row < rows) & (col >= 0) & (col < cols)
    start = (1.0 + 1.5 * demand / (1.0 + demand)) * area
    density = jnp.where(inside, start, 0.0)
    keep = jnp.where(inside, 0.04, 0.0)
    gain = jnp.where(inside, 0.24, 0.0)
    for _ in range(STEPS):
        beside = (
            pltpu.roll(density, 1, 0)
            + pltpu.roll(density, shape[0] - 1, 0)
            + pltpu.roll(density, 1, 1)
            + pltpu.roll(density, shape[1] - 1, 1)
        )
        density = keep * density + gain * beside
    density_out[...] = density[:BR, :BC]


def swap(block, axis, first):
    pairs = range(first, lax.axis_size(axis) - 1, 2)
    return lax.ppermute(block, axis, [p for i in pairs for p in ((i, i + 1), (i + 1, i))])


def call(kernel, shapes, *args, space=VMEM, scratch=()):
    return pl.pallas_call(
        kernel,
        out_shape=[jax.ShapeDtypeStruct(s, F32) for s in shapes],
        in_specs=[pl.BlockSpec(memory_space=space)] * len(args),
        out_specs=[pl.BlockSpec(memory_space=VMEM)] * len(shapes),
        scratch_shapes=list(scratch),
        compiler_params=pltpu.CompilerParams(vmem_limit_bytes=40 * 2**20),
    )(*args)


def body(boxes, pins, cell_bins, cell_area):
    pins = pins.reshape(-1, 128)
    cell_area = cell_area.reshape(-1, 128)
    inputs = (boxes, pins, cell_bins, cell_area)
    inputs = [pltpu.with_memory_space_constraint(a, HBM) for a in inputs]
    d_own, a_own, even, odd = call(
        window_kernel,
        [(BR + 8, WIDE), (BR, BC), (80, WIDE), (80, WIDE)],
        *inputs,
        space=HBM,
        scratch=[pltpu.VMEM(a.shape, a.dtype) for a in inputs]
        + [pltpu.VMEM(pins.shape, F32)] * 2
        + [pltpu.SemaphoreType.DMA((4,))],
    )
    odd = swap(odd, "row", 1)
    even = swap(even, "row", 0)
    d_ext, a_ext, even, odd = call(
        merge_kernel,
        [(BR + 16, WIDE), (BR + 16, BC), (BR + 48, 128), (BR + 48, 128)],
        d_own,
        a_own,
        even,
        odd,
    )
    odd = swap(odd, "col", 1)
    even = swap(even, "col", 0)
    demand, density = call(final_kernel, [(BR, BC), (BR, BC)], d_ext, a_ext, even, odd)
    return (demand, density)


def solution(mesh):
    return jax.shard_map(
        body,
        mesh=mesh,
        in_specs=(
            P(None, ("row", "col")),
            P(("row", "col")),
            P(None, ("row", "col")),
            P(("row", "col")),
        ),
        out_specs=(P("row", "col"), P("row", "col")),
        check_vma=False,
    )
```

```python
import jax
import jax.numpy as jnp
from jax import lax
from jax.experimental import pallas as pl
from jax.experimental.pallas import tpu as pltpu
from jax.sharding import PartitionSpec as P

BR = 128
BC = 256
STEPS = 6
TALL = 192
WIDE = 384
NET_BLOCK = 4096
CELL_BLOCK = 8192
FACTORS = 24
F32 = jnp.float32
BF16 = jnp.bfloat16
FP8 = jnp.float8_e4m3fn
VMEM = pltpu.MemorySpace.VMEM
HBM = pltpu.MemorySpace.HBM


def repeated(value, rows, dtype):
    if dtype != jnp.int8:
        value = value.astype(F32)
    return jnp.broadcast_to(value, (rows, value.shape[1])).astype(dtype)[None]


def ruler(length, rows, shift, n, dtype):
    shape = (length // rows, rows, n)
    place = lax.broadcasted_iota(jnp.int32, shape, 0) * rows
    place = place + lax.broadcasted_iota(jnp.int32, shape, 1) - shift
    return place.astype(dtype) if dtype == jnp.int8 else place.astype(F32).astype(dtype)


def lane_row(ref, first, n):
    return jnp.concatenate([ref[pl.ds(first // 128 + i, 1), :] for i in range(n // 128)], axis=1)


def nt_dot(left, right):
    return lax.dot_general(left, right, (((1,), (1,)), ((), ())), preferred_element_type=F32)


def split_weights(boxes, pins, row_factor, col_factor):
    width = boxes[3:4, :] - boxes[2:3, :] + 1
    height = boxes[1:2, :] - boxes[0:1, :] + 1
    nets = width.shape[1]
    width, height = (
        jnp.concatenate([v[:, i : i + 128] for i in range(0, nets, 128)], axis=0).astype(F32)
        for v in (width, height)
    )
    weight = pins[...].astype(F32) * (width + height) / (width * height) * (1.0 / 16.0)
    best = weight
    for k in range(FACTORS):
        one = 1.0 + k / 128.0
        other = (weight * (1.0 / one)).astype(BF16).astype(F32)
        error = jnp.abs(other * one - weight)
        if k == 0:
            best, row_part, col_part = error, jnp.ones_like(weight), other
        else:
            better = error < best
            best = jnp.where(better, error, best)
            row_part = jnp.where(better, one, row_part)
            col_part = jnp.where(better, other, col_part)
    row_factor[...] = row_part
    col_factor[...] = col_part


def window_kernel(
    boxes_in, pins_in, bins_in, area_in, d_out, a_out, even_out, odd_out,
    boxes, pins, bins, area, row_factor, col_factor, sems,
):
    copies = [
        pltpu.make_async_copy(source, target, sems.at[i])
        for i, (source, target) in enumerate(
            ((boxes_in, boxes), (pins_in, pins), (bins_in, bins), (area_in, area))
        )
    ]
    for copy in copies:
        copy.start()
    copies[0].wait()
    copies[1].wait()
    split_weights(boxes, pins, row_factor, col_factor)
    n = NET_BLOCK
    zero = jnp.zeros((), BF16)

    def add_nets(i, demand):
        k = pl.multiple_of(i * n, n)
        box = boxes[:, pl.ds(k, n)]
        y0, y1, x0, x1 = (box[i : i + 1] for i in range(4))
        top = y0 & (BR - 1)
        bottom = y1 - (y0 - top)
        start = x0 & (BC - 1)
        end = x1 - (x0 - start)
        rows = ruler(TALL, 16, 0, n, BF16)
        inside = (rows >= repeated(top, 16, BF16)) & (rows <= repeated(bottom, 16, BF16))
        down = jnp.where(inside, repeated(lane_row(row_factor, k, n), 16, BF16), zero)
        cols = ruler(WIDE, 16, 192, n, BF16)
        inside = (cols >= repeated(start - 192, 16, BF16)) & (
            cols <= repeated(end - 192, 16, BF16)
        )
        right = jnp.where(inside, repeated(lane_row(col_factor, k, n), 16, BF16), zero)
        return demand + nt_dot(right.reshape(WIDE, n), down.reshape(TALL, n))

    demand = lax.fori_loop(0, boxes.shape[1] // n, add_nets, jnp.zeros((WIDE, TALL), F32))
    copies[2].wait()
    copies[3].wait()
    m = CELL_BLOCK
    zero = jnp.zeros((), FP8)
    one = jnp.ones((), FP8)

    def add_cells(i, total):
        k = pl.multiple_of(i * m, m)
        where = bins[:, pl.ds(k, m)]
        size = lane_row(area, k, m)
        rows = ruler(BR, 32, 0, m, jnp.int8) == repeated(where[0:1] & (BR - 1), 32, jnp.int8)
        down = jnp.concatenate(
            [
                jnp.where(rows, repeated(part, 32, FP8), zero).reshape(BR, m)
                for part in (size >> 3, size & 7)
            ],
            axis=0,
        )
        cols = ruler(BC, 32, 128, m, jnp.int8) == repeated(
            (where[1:2] & (BC - 1)) - 128, 32, jnp.int8
        )
        right = jnp.where(cols, one, zero).reshape(BC, m)
        return total + nt_dot(right, down)

    total = lax.fori_loop(0, bins.shape[1] // m, add_cells, jnp.zeros((BC, 2 * BR), F32))
    demand = demand.T
    total = (total[:, :BR] * 0.5 + total[:, BR:] * (1.0 / 16.0)).T
    d_out[...] = demand[: BR + 8]
    a_out[...] = total
    even = lax.rem(lax.axis_index("row"), 2) == 0
    for message, goes_down in ((even_out, even), (odd_out, jnp.logical_not(even))):
        message[:8] = jnp.where(goes_down, demand[BR : BR + 8], demand[:8])
        message[8:64] = demand[BR + 8 :]
        message[64:72] = demand[BR - 8 : BR]
        message[72:, :BC] = jnp.where(goes_down, total[BR - 8 :], total[:8])


def merge_kernel(d_own, a_own, odd_in, even_in, d_out, a_out, even_out, odd_out):
    even = lax.rem(lax.axis_index("row"), 2) == 0
    above = jnp.where(even, odd_in[...], even_in[...])
    below = jnp.where(even, even_in[:8], odd_in[:8])
    below_area = jnp.where(even, even_in[72:, :BC], odd_in[72:, :BC])
    demand = jnp.concatenate(
        [d_own[:64] + above[:64], d_own[64:BR], d_own[BR:] + below, above[64:72]], axis=0
    )
    area = jnp.concatenate([a_own[...], below_area, above[72:, :BC]], axis=0)
    d_out[...] = demand
    a_out[...] = area
    lane = lax.broadcasted_iota(jnp.int32, (BR + 16, 128), 1)
    leftward = jnp.where(lane < 8, demand[:, :128], pltpu.roll(area[:, :128], 8, 1))
    strip = jnp.where(lane < 120, pltpu.roll(demand[:, 128:BC], 120, 1), area[:, 128:])
    strip = jnp.concatenate([strip, jnp.zeros((112, 128), F32)], axis=0).T[112:]
    even = lax.rem(lax.axis_index("col"), 2) == 0
    for message, goes_right in ((even_out, even), (odd_out, jnp.logical_not(even))):
        message[: BR + 16] = jnp.where(goes_right, demand[:, BC:], leftward)
        message[BR + 16 : BR + 32] = strip[:, :128]
        message[BR + 32 :] = strip[:, 128:]


def final_kernel(
    d_in, a_in, odd_in, even_in, demand_out, density_out, whole, own, field, inner, sems
):
    tall = BR + 16
    even = lax.rem(lax.axis_index("col"), 2) == 0
    left = jnp.where(even, odd_in[...], even_in[...])
    right = jnp.where(even, even_in[:tall], odd_in[:tall])
    strip = jnp.concatenate([left[tall : tall + 16], left[tall + 16 :]], axis=1)
    strip = jnp.concatenate([jnp.zeros((112, 256), F32), strip], axis=0).T[:tall]
    lane = lax.broadcasted_iota(jnp.int32, (tall, 128), 1)
    beyond = jnp.where(lane < 8, d_in[:, BC:] + right, pltpu.roll(strip, 8, 1))
    demand = jnp.concatenate([d_in[:, :128] + left[:tall], d_in[:, 128:BC], beyond], axis=1)
    beyond = jnp.where(lane < 8, pltpu.roll(right, 120, 1), strip)
    area = jnp.concatenate([a_in[...], beyond], axis=1)
    whole[...] = demand[:BR, :BC]
    sent = pltpu.make_async_copy(whole, demand_out, sems.at[0])
    sent.start()
    shape = demand.shape
    row = lax.broadcasted_iota(jnp.int32, shape, 0)
    row = jnp.where(row < BR + 8, row, row - tall) + lax.axis_index("row") * BR
    lane = lax.broadcasted_iota(jnp.int32, shape, 1)
    near = (lane < BC + 8) | (lane >= WIDE - 8)
    col = jnp.where(lane < BC + 8, lane, lane - WIDE) + lax.axis_index("col") * BC
    rows, cols = lax.axis_size("row") * BR, lax.axis_size("col") * BC
    inside = near & (row >= 0) & (row < rows) & (col >= 0) & (col < cols)
    start = (1.0 + 1.5 * demand / (1.0 + demand)) * area
    density = jnp.where(inside, start, 0.0)
    mask = jnp.where(inside, 1.0, 0.0)
    for i in range(3):
        field[i] = density[:, 128 * i : 128 * (i + 1)]
        inner[i] = mask[:, 128 * i : 128 * (i + 1)]
    part = shape[0] // 8

    def strided(ref, k):
        return jnp.concatenate([ref[i, pl.ds(k, 8, stride=part), :] for i in range(3)], axis=1)

    block = [strided(field, k) for k in range(part)]

    def step(_, block):
        first = pltpu.roll(block[-1], 1, 0)
        last = pltpu.roll(block[0], 7, 0)
        rows = [first, *block, last]
        new = []
        for k in range(part):
            mid = rows[k + 1]
            beside = rows[k] + rows[k + 2] + pltpu.roll(mid, 1, 1) + pltpu.roll(mid, WIDE - 1, 1)
            new.append(strided(inner, k) * (0.04 * mid + 0.24 * beside))
        return tuple(new)

    for _ in range(STEPS):
        block = step(0, block)
    for k in range(part):
        for i in range(2):
            field[i, pl.ds(k, 8, stride=part), :] = block[k][:, 128 * i : 128 * (i + 1)]
    for i in range(2):
        own[:, 128 * i : 128 * (i + 1)] = field[i, :BR]
    last = pltpu.make_async_copy(own, density_out, sems.at[1])
    last.start()
    last.wait()
    sent.wait()


def swap(block, axis, first):
    pairs = range(first, lax.axis_size(axis) - 1, 2)
    return lax.ppermute(block, axis, [p for i in pairs for p in ((i, i + 1), (i + 1, i))])


def call(kernel, shapes, *args, space=VMEM, scratch=()):
    return pl.pallas_call(
        kernel,
        out_shape=[jax.ShapeDtypeStruct(s, F32) for s in shapes],
        in_specs=[pl.BlockSpec(memory_space=space)] * len(args),
        out_specs=[pl.BlockSpec(memory_space=VMEM)] * len(shapes),
        scratch_shapes=list(scratch),
        compiler_params=pltpu.CompilerParams(vmem_limit_bytes=40 * 2**20),
    )(*args)


def body(boxes, pins, cell_bins, cell_area):
    pins = pins.reshape(-1, 128)
    cell_area = cell_area.reshape(-1, 128)
    inputs = (boxes, pins, cell_bins, cell_area)
    inputs = [pltpu.with_memory_space_constraint(a, HBM) for a in inputs]
    d_own, a_own, even, odd = call(
        window_kernel,
        [(BR + 8, WIDE), (BR, BC), (80, WIDE), (80, WIDE)],
        *inputs,
        space=HBM,
        scratch=[pltpu.VMEM(a.shape, a.dtype) for a in inputs]
        + [pltpu.VMEM(pins.shape, F32)] * 2
        + [pltpu.SemaphoreType.DMA((4,))],
    )
    odd = swap(odd, "row", 1)
    even = swap(even, "row", 0)
    d_ext, a_ext, even, odd = call(
        merge_kernel,
        [(BR + 16, WIDE), (BR + 16, BC), (BR + 48, 128), (BR + 48, 128)],
        d_own,
        a_own,
        odd,
        even,
    )
    odd = swap(odd, "col", 1)
    even = swap(even, "col", 0)
    demand, density = pl.pallas_call(
        final_kernel,
        out_shape=[jax.ShapeDtypeStruct((BR, BC), F32)] * 2,
        in_specs=[pl.BlockSpec(memory_space=VMEM)] * 4,
        out_specs=[pl.BlockSpec(memory_space=HBM)] * 2,
        scratch_shapes=[
            pltpu.VMEM((BR, BC), F32),
            pltpu.VMEM((BR, BC), F32),
            pltpu.VMEM((3, BR + 16, 128), F32),
            pltpu.VMEM((3, BR + 16, 128), F32),
            pltpu.SemaphoreType.DMA((2,)),
        ],
        compiler_params=pltpu.CompilerParams(vmem_limit_bytes=40 * 2**20),
    )(d_ext, a_ext, odd, even)
    return (demand, density)


def solution(mesh):
    return jax.shard_map(
        body,
        mesh=mesh,
        in_specs=(
            P(None, ("row", "col")),
            P(("row", "col")),
            P(None, ("row", "col")),
            P(("row", "col")),
        ),
        out_specs=(P("row", "col"), P("row", "col")),
        check_vma=False,
    )
```

```python
import jax
import jax.numpy as jnp
from jax import lax
from jax.experimental import pallas as pl
from jax.experimental.pallas import tpu as pltpu
from jax.sharding import PartitionSpec as P

BR = 128
BC = 256
STEPS = 6
PART = (BR + 16) // 8
TALL = 192
WIDE = 384
NET_BLOCK = 4096
CELL_BLOCK = 8192
FACTORS = 24
F32 = jnp.float32
BF16 = jnp.bfloat16
FP8 = jnp.float8_e4m3fn
VMEM = pltpu.MemorySpace.VMEM
HBM = pltpu.MemorySpace.HBM


def repeated(value, rows, dtype):
    if dtype != jnp.int8:
        value = value.astype(F32)
    return jnp.broadcast_to(value, (rows, value.shape[1])).astype(dtype)[None]


def ruler(length, rows, shift, n, dtype):
    shape = (length // rows, rows, n)
    place = lax.broadcasted_iota(jnp.int32, shape, 0) * rows
    place = place + lax.broadcasted_iota(jnp.int32, shape, 1) - shift
    return place.astype(dtype) if dtype == jnp.int8 else place.astype(F32).astype(dtype)


def lane_row(ref, first, n):
    return jnp.concatenate([ref[pl.ds(first // 128 + i, 1), :] for i in range(n // 128)], axis=1)


def nt_dot(left, right):
    return lax.dot_general(left, right, (((1,), (1,)), ((), ())), preferred_element_type=F32)


def split_weights(boxes, pins, row_factor, col_factor):
    width = boxes[3:4, :] - boxes[2:3, :] + 1
    height = boxes[1:2, :] - boxes[0:1, :] + 1
    nets = width.shape[1]
    width, height = (
        jnp.concatenate([v[:, i : i + 128] for i in range(0, nets, 128)], axis=0).astype(F32)
        for v in (width, height)
    )
    weight = pins[...].astype(F32) * (width + height) / (width * height) * (1.0 / 16.0)
    best = weight
    for k in range(FACTORS):
        one = 1.0 + k / 128.0
        other = (weight * (1.0 / one)).astype(BF16).astype(F32)
        error = jnp.abs(other * one - weight)
        if k == 0:
            best, row_part, col_part = error, jnp.ones_like(weight), other
        else:
            better = error < best
            best = jnp.where(better, error, best)
            row_part = jnp.where(better, one, row_part)
            col_part = jnp.where(better, other, col_part)
    row_factor[...] = row_part
    col_factor[...] = col_part


def window_kernel(
    boxes_in, pins_in, bins_in, area_in, d_out, a_out, even_out, odd_out,
    boxes, pins, bins, area, row_factor, col_factor, sems,
):
    copies = [
        pltpu.make_async_copy(source, target, sems.at[i])
        for i, (source, target) in enumerate(
            ((boxes_in, boxes), (pins_in, pins), (bins_in, bins), (area_in, area))
        )
    ]
    for copy in copies:
        copy.start()
    copies[0].wait()
    copies[1].wait()
    split_weights(boxes, pins, row_factor, col_factor)
    n = NET_BLOCK
    zero = jnp.zeros((), BF16)

    def add_nets(i, demand):
        k = i * n
        box = boxes[:, pl.ds(k, n)]
        y0, y1, x0, x1 = (box[i : i + 1] for i in range(4))
        top = y0 & (BR - 1)
        bottom = y1 - (y0 - top)
        start = x0 & (BC - 1)
        end = x1 - (x0 - start)
        rows = ruler(TALL, 16, 0, n, BF16)
        inside = (rows >= repeated(top, 16, BF16)) & (rows <= repeated(bottom, 16, BF16))
        down = jnp.where(inside, repeated(lane_row(row_factor, k, n), 16, BF16), zero)
        cols = ruler(WIDE, 16, 192, n, BF16)
        inside = (cols >= repeated(start - 192, 16, BF16)) & (
            cols <= repeated(end - 192, 16, BF16)
        )
        right = jnp.where(inside, repeated(lane_row(col_factor, k, n), 16, BF16), zero)
        return demand + nt_dot(right.reshape(WIDE, n), down.reshape(TALL, n))

    demand = add_nets(0, jnp.zeros((WIDE, TALL), F32))
    copies[2].wait()
    copies[3].wait()
    m = CELL_BLOCK
    zero = jnp.zeros((), FP8)
    one = jnp.ones((), FP8)

    def add_cells(i, total):
        k = pl.multiple_of(i * m, m)
        where = bins[:, pl.ds(k, m)]
        size = lane_row(area, k, m)
        rows = ruler(BR, 32, 0, m, jnp.int8) == repeated(where[0:1] & (BR - 1), 32, jnp.int8)
        down = jnp.concatenate(
            [
                jnp.where(rows, repeated(part, 32, FP8), zero).reshape(BR, m)
                for part in (size >> 3, size & 7)
            ],
            axis=0,
        )
        cols = ruler(BC, 32, 128, m, jnp.int8) == repeated(
            (where[1:2] & (BC - 1)) - 128, 32, jnp.int8
        )
        right = jnp.where(cols, one, zero).reshape(BC, m)
        return total + nt_dot(down, right)

    total = lax.fori_loop(0, bins.shape[1] // m, add_cells, jnp.zeros((2 * BR, BC), F32))
    demand = demand.T
    total = total[:BR] * 0.5 + total[BR:] * (1.0 / 16.0)
    d_out[...] = demand[: BR + 8]
    a_out[...] = total
    even = lax.rem(lax.axis_index("row"), 2) == 0
    for message, goes_down in ((even_out, even), (odd_out, jnp.logical_not(even))):
        message[:8] = jnp.where(goes_down, demand[BR : BR + 8], demand[:8])
        message[8:64] = demand[BR + 8 :]
        message[64:72] = demand[BR - 8 : BR]
        message[72:, :BC] = jnp.where(goes_down, total[BR - 8 :], total[:8])


def merge_kernel(d_own, a_own, odd_in, even_in, d_out, a_out, right_out, left_out):
    even = lax.rem(lax.axis_index("row"), 2) == 0
    above = jnp.where(even, odd_in[...], even_in[...])
    below = jnp.where(even, even_in[:8], odd_in[:8])
    below_area = jnp.where(even, even_in[72:, :BC], odd_in[72:, :BC])
    demand = jnp.concatenate(
        [d_own[:64] + above[:64], d_own[64:BR], d_own[BR:] + below, above[64:72]], axis=0
    )
    area = jnp.concatenate([a_own[...], below_area, above[72:, :BC]], axis=0)
    d_out[...] = demand
    a_out[...] = area
    lane = lax.broadcasted_iota(jnp.int32, (BR + 16, 128), 1)
    first = jnp.where(lane < 8, demand[:, :128], pltpu.roll(area[:, :128], 8, 1))
    strip = jnp.where(lane < 120, pltpu.roll(demand[:, 128:BC], 120, 1), area[:, 128:])
    strip = jnp.where(lane < 16, first, strip)
    strip = jnp.concatenate([strip, jnp.zeros((112, 128), F32)], axis=0).T
    right_out[: BR + 16] = demand[:, BC:]
    right_out[BR + 16 : BR + 32] = strip[112:, :128]
    right_out[BR + 32 :] = strip[112:, 128:]
    left_out[:16] = strip[:16, :128]
    left_out[16:] = strip[:16, 128:]


def inside_of(col):
    row = lax.broadcasted_iota(jnp.int32, col.shape, 0)
    row = jnp.where(row < BR + 8, row, row - (BR + 16)) + lax.axis_index("row") * BR
    col = col + lax.axis_index("col") * BC
    rows, cols = lax.axis_size("row") * BR, lax.axis_size("col") * BC
    inside = (row >= 0) & (row < rows) & (col >= 0) & (col < cols)
    return jnp.where(inside, 1.0, 0.0)


def inflated(demand, area):
    return (1.0 + 1.5 * demand / (1.0 + demand)) * area


def blocks_of(value, field):
    for i in range(2):
        field[i] = value[:, 128 * i : 128 * (i + 1)]
    return [
        jnp.concatenate([field[i, pl.ds(k, 8, stride=PART), :] for i in range(2)], axis=1)
        for k in range(PART)
    ]


def diffused(block, inner):
    for _ in range(STEPS):
        rows = [pltpu.roll(block[-1], 1, 0), *block, pltpu.roll(block[0], 7, 0)]
        block = []
        for k in range(PART):
            mid = rows[k + 1]
            beside = rows[k] + rows[k + 2] + pltpu.roll(mid, 1, 1) + pltpu.roll(mid, 255, 1)
            block.append(inner(k) * (0.04 * mid + 0.24 * beside))
    return block


def half_kernel(d_in, a_in, spread_out, mask_out, field):
    lane = lax.broadcasted_iota(jnp.int32, (BR + 16, BC), 1)
    col = jnp.where(lane < 160, lane, jnp.where(lane < 224, lane + 64, lane - BC))
    for k, block in enumerate(blocks_of(inside_of(col), field)):
        mask_out[8 * k : 8 * k + 8] = block
    mask = inside_of(jnp.where(lane < 64, lane + BC, lane))
    mask = blocks_of(mask, field)
    start = inflated(d_in[:, 128:BC], a_in[:, 128:]) * inside_of(lane[:, 128:])
    start = jnp.concatenate([jnp.zeros((BR + 16, 128), F32), start], axis=1)
    block = diffused(blocks_of(start, field), lambda k: mask[k])
    for k in range(PART):
        spread_out[8 * k : 8 * k + 8] = jnp.where(lane[:8] < 64, 0.0, block[k])


def final_kernel(
    d_in, a_in, half, mask, left, right, demand_out, density_out, own, field, sems
):
    tall = BR + 16
    strip = jnp.concatenate(
        [
            jnp.concatenate([right[:16], right[16:]], axis=1),
            jnp.zeros((96, 256), F32),
            jnp.concatenate([left[tall : tall + 16], left[tall + 16 :]], axis=1),
        ],
        axis=0,
    ).T[:tall]
    low = d_in[:, :128] + left[:tall]
    own[...] = low[:BR]
    copies = [
        pltpu.make_async_copy(own, demand_out.at[:, :128], sems.at[0]),
        pltpu.make_async_copy(d_in.at[:BR, 128:BC], demand_out.at[:, 128:], sems.at[1]),
    ]
    for copy in copies:
        copy.start()
    lane = lax.broadcasted_iota(jnp.int32, (tall, 128), 1)
    demand = pltpu.roll(jnp.where(lane < 8, d_in[:, BC:] + strip, 0.0), 64, 1)
    demand = jnp.where(lane < 120, demand, pltpu.roll(strip, 8, 1))
    used = ((lane >= 64) & (lane < 72)) | (lane >= 120)
    area = jnp.where(lane < 120, pltpu.roll(strip, 56, 1), strip)
    start = inflated(demand, jnp.where(used, area, 0.0))
    start = jnp.concatenate([inflated(low, a_in[:, :128]), start], axis=1)
    block = blocks_of(start, field)

    def inner(k):
        return mask[8 * k : 8 * k + 8]

    block = diffused([inner(k) * block[k] for k in range(PART)], inner)
    lane = lane[:8]
    for k in range(PART):
        known = half[8 * k : 8 * k + 8]
        field[0, pl.ds(k, 8, stride=PART), :] = block[k][:, :128] + known[:, :128]
        more = block[k][:, 128:]
        more = jnp.where(lane < 32, more, jnp.where(lane >= 96, pltpu.roll(more, 64, 1), 0.0))
        field[1, pl.ds(k, 8, stride=PART), :] = more + known[:, 128:]
    for i in range(2):
        copies.append(
            pltpu.make_async_copy(
                field.at[i, :BR], density_out.at[:, 128 * i : 128 * (i + 1)], sems.at[2 + i]
            )
        )
        copies[-1].start()
    for copy in copies:
        copy.wait()


def swap(block, axis, first):
    pairs = range(first, lax.axis_size(axis) - 1, 2)
    return lax.ppermute(block, axis, [p for i in pairs for p in ((i, i + 1), (i + 1, i))])


def shift(block, axis, distance):
    devices = range(lax.axis_size(axis))
    route = [(i, i + distance) for i in devices if i + distance in devices]
    return lax.ppermute(block, axis, route)


def call(kernel, shapes, *args, space=VMEM, scratch=()):
    return pl.pallas_call(
        kernel,
        out_shape=[jax.ShapeDtypeStruct(s, F32) for s in shapes],
        in_specs=[pl.BlockSpec(memory_space=space)] * len(args),
        out_specs=[pl.BlockSpec(memory_space=VMEM)] * len(shapes),
        scratch_shapes=list(scratch),
        compiler_params=pltpu.CompilerParams(vmem_limit_bytes=40 * 2**20),
    )(*args)


def body(boxes, pins, cell_bins, cell_area):
    pins = pins.reshape(-1, 128)
    cell_area = cell_area.reshape(-1, 128)
    inputs = (boxes, pins, cell_bins, cell_area)
    inputs = [pltpu.with_memory_space_constraint(a, HBM) for a in inputs]
    d_own, a_own, even, odd = call(
        window_kernel,
        [(BR + 8, WIDE), (BR, BC), (80, WIDE), (80, WIDE)],
        *inputs,
        space=HBM,
        scratch=[pltpu.VMEM(a.shape, a.dtype) for a in inputs]
        + [pltpu.VMEM(pins.shape, F32)] * 2
        + [pltpu.SemaphoreType.DMA((4,))],
    )
    odd = swap(odd, "row", 1)
    even = swap(even, "row", 0)
    d_ext, a_ext, right, left = call(
        merge_kernel,
        [(BR + 16, WIDE), (BR + 16, BC), (BR + 48, 128), (32, 128)],
        d_own,
        a_own,
        odd,
        even,
    )
    left, right = shift(right, "col", 1), shift(left, "col", -1)
    half, mask = call(
        half_kernel,
        [(BR + 16, BC), (BR + 16, BC)],
        d_ext,
        a_ext,
        scratch=[pltpu.VMEM((2, BR + 16, 128), F32)],
    )
    demand, density = pl.pallas_call(
        final_kernel,
        out_shape=[jax.ShapeDtypeStruct((BR, BC), F32)] * 2,
        in_specs=[pl.BlockSpec(memory_space=VMEM)] * 6,
        out_specs=[pl.BlockSpec(memory_space=HBM)] * 2,
        scratch_shapes=[
            pltpu.VMEM((BR, 128), F32),
            pltpu.VMEM((2, BR + 16, 128), F32),
            pltpu.SemaphoreType.DMA((4,)),
        ],
        compiler_params=pltpu.CompilerParams(vmem_limit_bytes=40 * 2**20),
    )(d_ext, a_ext, half, mask, left, right)
    return (demand, density)


def solution(mesh):
    return jax.shard_map(
        body,
        mesh=mesh,
        in_specs=(
            P(None, ("row", "col")),
            P(("row", "col")),
            P(None, ("row", "col")),
            P(("row", "col")),
        ),
        out_specs=(P("row", "col"), P("row", "col")),
        check_vma=False,
    )
```

```python
import jax
import jax.numpy as jnp
from jax import lax
from jax.experimental import pallas as pl
from jax.experimental.pallas import tpu as pltpu
from jax.sharding import PartitionSpec as P

BR = 128
BC = 256
STEPS = 6
PART = (BR + 16) // 8
TALL = 192
WIDE = 384
NET_BLOCK = 4096
CELL_BLOCK = 8192
FACTORS = 24
F32 = jnp.float32
BF16 = jnp.bfloat16
FP8 = jnp.float8_e4m3fn
VMEM = pltpu.MemorySpace.VMEM
HBM = pltpu.MemorySpace.HBM


def repeated(value, rows, dtype):
    if dtype != jnp.int8:
        value = value.astype(F32)
    return jnp.broadcast_to(value, (rows, value.shape[1])).astype(dtype)[None]


def ruler(length, rows, shift, n, dtype):
    shape = (length // rows, rows, n)
    place = lax.broadcasted_iota(jnp.int32, shape, 0) * rows
    place = place + lax.broadcasted_iota(jnp.int32, shape, 1) - shift
    return place.astype(dtype) if dtype == jnp.int8 else place.astype(F32).astype(dtype)


def lane_row(ref, first, n):
    return jnp.concatenate([ref[pl.ds(first // 128 + i, 1), :] for i in range(n // 128)], axis=1)


def nt_dot(left, right):
    return lax.dot_general(left, right, (((1,), (1,)), ((), ())), preferred_element_type=F32)


def split_weights(boxes, pins, row_factor, col_factor):
    width = boxes[3:4, :] - boxes[2:3, :] + 1
    height = boxes[1:2, :] - boxes[0:1, :] + 1
    nets = width.shape[1]
    width, height = (
        jnp.concatenate([v[:, i : i + 128] for i in range(0, nets, 128)], axis=0).astype(F32)
        for v in (width, height)
    )
    weight = pins[...].astype(F32) * (width + height) / (width * height) * (1.0 / 16.0)
    best = weight
    for k in range(FACTORS):
        one = 1.0 + k / 128.0
        other = (weight * (1.0 / one)).astype(BF16).astype(F32)
        error = jnp.abs(other * one - weight)
        if k == 0:
            best, row_part, col_part = error, jnp.ones_like(weight), other
        else:
            better = error < best
            best = jnp.where(better, error, best)
            row_part = jnp.where(better, one, row_part)
            col_part = jnp.where(better, other, col_part)
    row_factor[...] = row_part
    col_factor[...] = col_part


def window_kernel(
    boxes_in, pins_in, bins_in, area_in, d_out, a_out, even_out, odd_out,
    boxes, pins, bins, area, row_factor, col_factor, sems,
):
    copies = [
        pltpu.make_async_copy(source, target, sems.at[i])
        for i, (source, target) in enumerate(
            ((boxes_in, boxes), (pins_in, pins), (bins_in, bins), (area_in, area))
        )
    ]
    for copy in copies:
        copy.start()
    copies[0].wait()
    copies[1].wait()
    split_weights(boxes, pins, row_factor, col_factor)
    n = NET_BLOCK
    zero = jnp.zeros((), BF16)

    def add_nets(i, demand):
        k = i * n
        box = boxes[:, pl.ds(k, n)]
        y0, y1, x0, x1 = (box[i : i + 1] for i in range(4))
        top = y0 & (BR - 1)
        bottom = y1 - (y0 - top)
        start = x0 & (BC - 1)
        end = x1 - (x0 - start)
        rows = ruler(TALL, 16, 0, n, BF16)
        inside = (rows >= repeated(top, 16, BF16)) & (rows <= repeated(bottom, 16, BF16))
        down = jnp.where(inside, repeated(lane_row(row_factor, k, n), 16, BF16), zero)
        cols = ruler(WIDE, 16, 192, n, BF16)
        inside = (cols >= repeated(start - 192, 16, BF16)) & (
            cols <= repeated(end - 192, 16, BF16)
        )
        right = jnp.where(inside, repeated(lane_row(col_factor, k, n), 16, BF16), zero)
        return demand + nt_dot(right.reshape(WIDE, n), down.reshape(TALL, n))

    demand = add_nets(0, jnp.zeros((WIDE, TALL), F32))
    copies[2].wait()
    copies[3].wait()
    m = CELL_BLOCK
    zero = jnp.zeros((), FP8)
    one = jnp.ones((), FP8)

    def add_cells(i, total):
        k = pl.multiple_of(i * m, m)
        where = bins[:, pl.ds(k, m)]
        size = lane_row(area, k, m)
        rows = ruler(BR, 32, 0, m, jnp.int8) == repeated(where[0:1] & (BR - 1), 32, jnp.int8)
        down = jnp.concatenate(
            [
                jnp.where(rows, repeated(part, 32, FP8), zero).reshape(BR, m)
                for part in (size >> 3, size & 7)
            ],
            axis=0,
        )
        cols = ruler(BC, 32, 128, m, jnp.int8) == repeated(
            (where[1:2] & (BC - 1)) - 128, 32, jnp.int8
        )
        right = jnp.where(cols, one, zero).reshape(BC, m)
        return total + nt_dot(down, right)

    total = lax.fori_loop(0, bins.shape[1] // m, add_cells, jnp.zeros((2 * BR, BC), F32))
    demand = demand.T
    total = total[:BR] * 0.5 + total[BR:] * (1.0 / 16.0)
    d_out[...] = demand[: BR + 8]
    a_out[...] = total
    even = lax.rem(lax.axis_index("row"), 2) == 0
    for message, goes_down in ((even_out, even), (odd_out, jnp.logical_not(even))):
        message[:8] = jnp.where(goes_down, demand[BR : BR + 8], demand[:8])
        message[8:64] = demand[BR + 8 :]
        message[64:72] = demand[BR - 8 : BR]
        message[72:, :BC] = jnp.where(goes_down, total[BR - 8 :], total[:8])


def lying(strip):
    gap = jnp.zeros((112, 128), F32)
    return jnp.concatenate([strip[: BR + 8], gap, strip[BR + 8 :]], axis=0).T


def merge_kernel(d_own, a_own, odd_in, even_in, d_out, a_out, right_out, left_out):
    even = lax.rem(lax.axis_index("row"), 2) == 0
    above = jnp.where(even, odd_in[...], even_in[...])
    below = jnp.where(even, even_in[:8], odd_in[:8])
    below_area = jnp.where(even, even_in[72:, :BC], odd_in[72:, :BC])
    demand = jnp.concatenate(
        [d_own[:64] + above[:64], d_own[64:BR], d_own[BR:] + below, above[64:72]], axis=0
    )
    area = jnp.concatenate([a_own[...], below_area, above[72:, :BC]], axis=0)
    d_out[...] = demand
    a_out[...] = area
    lane = lax.broadcasted_iota(jnp.int32, (BR + 16, 128), 1)
    first = jnp.where(lane < 8, demand[:, :128], pltpu.roll(area[:, :128], 8, 1))
    strip = jnp.where(lane < 120, pltpu.roll(demand[:, 128:BC], 120, 1), area[:, 128:])
    strip = jnp.where(lane < 16, first, strip)
    strip = lying(strip)
    right_out[: BR + 16] = demand[:, BC:]
    right_out[BR + 16 : BR + 32] = strip[112:, :128]
    right_out[BR + 32 :] = strip[112:, 128:]
    left_out[:16] = strip[:16, :128]
    left_out[16:] = strip[:16, 128:]


def inside_of(col):
    row = lax.broadcasted_iota(jnp.int32, col.shape, 0)
    row = jnp.where(row < BR + 8, row, row - (BR + 16)) + lax.axis_index("row") * BR
    col = col + lax.axis_index("col") * BC
    rows, cols = lax.axis_size("row") * BR, lax.axis_size("col") * BC
    inside = (row >= 0) & (row < rows) & (col >= 0) & (col < cols)
    return jnp.where(inside, 1.0, 0.0)


def inflated(demand, area):
    return (1.0 + 1.5 * demand / (1.0 + demand)) * area


def blocks_of(value, field):
    tiles = range(value.shape[1] // 128)
    for i in tiles:
        field[i] = value[:, 128 * i : 128 * (i + 1)]
    return [
        jnp.concatenate([field[i, pl.ds(k, 8, stride=PART), :] for i in tiles], axis=1)
        for k in range(PART)
    ]


def diffused(block, inner):
    wide = block[0].shape[1]
    for _ in range(STEPS):
        rows = [pltpu.roll(block[-1], 1, 0), *block, pltpu.roll(block[0], 7, 0)]
        block = []
        for k in range(PART):
            mid = rows[k + 1]
            beside = rows[k] + rows[k + 2] + pltpu.roll(mid, 1, 1) + pltpu.roll(mid, wide - 1, 1)
            block.append(inner(k) * (0.04 * mid + 0.24 * beside))
    return block


def upright(strip):
    strip = jnp.concatenate([strip[:16], strip[16:]], axis=1)
    strip = jnp.concatenate([jnp.zeros((112, 256), F32), strip], axis=0).T
    return jnp.concatenate([strip[: BR + 8], strip[248:]], axis=0)


def middle_kernel(d_in, a_in, spread_out, mask_out, over_out, field):
    lane = lax.broadcasted_iota(jnp.int32, (BR + 16, BC), 1)
    for k, block in enumerate(blocks_of(inside_of(jnp.where(lane < 192, lane, lane - BC)), field)):
        mask_out[8 * k : 8 * k + 8] = block
    over_out[...] = lying(d_in[:, BC:])[:8]
    mask = blocks_of(inside_of(jnp.where(lane < 64, lane + BC, lane)), field)
    start = inflated(d_in[:, 128:BC], a_in[:, 128:]) * inside_of(lane[:, 128:])
    start = jnp.concatenate([jnp.zeros((BR + 16, 128), F32), start], axis=1)
    block = diffused(blocks_of(start, field), lambda k: mask[k])
    for k in range(PART):
        spread_out[8 * k : 8 * k + 8] = jnp.where(lane[:8] < 64, 0.0, block[k])


def low_kernel(d_in, a_in, spread, mask, left, demand_out, spread_out, own, field, sems):
    tall = BR + 16
    low = d_in[:, :128] + left[:tall]
    own[...] = low[:BR]
    copies = [
        pltpu.make_async_copy(own, demand_out.at[:, :128], sems.at[0]),
        pltpu.make_async_copy(d_in.at[:BR, 128:BC], demand_out.at[:, 128:], sems.at[1]),
    ]
    for copy in copies:
        copy.start()
    strip = upright(left[tall:])
    lane = lax.broadcasted_iota(jnp.int32, (tall, 128), 1)
    start = jnp.where(lane >= 120, inflated(pltpu.roll(strip, 8, 1), strip), 0.0)
    start = jnp.concatenate([inflated(low, a_in[:, :128]), start], axis=1)
    block = blocks_of(start, field)

    def inner(k):
        return mask[8 * k : 8 * k + 8]

    block = diffused([inner(k) * block[k] for k in range(PART)], inner)
    lane = lax.broadcasted_iota(jnp.int32, (8, BC), 1)
    for k in range(PART):
        known = jnp.where(lane < 192, block[k], 0.0) + spread[8 * k : 8 * k + 8]
        for i in range(2):
            part = known[:, 128 * i : 128 * (i + 1)]
            spread_out[i, pl.ds(k, 8, stride=PART), :] = part
    for copy in copies:
        copy.wait()


def edge_kernel(spread, over, right, density_out, own, sems):
    first = pltpu.make_async_copy(spread.at[0, :BR], density_out.at[:, :128], sems.at[0])
    first.start()
    strip = jnp.concatenate([right[:16], right[16:]], axis=1)
    start = inflated(strip[:8] + over[...], strip[8:])
    none = jnp.zeros((8, 256), F32)
    density = jnp.concatenate([none, start, none], axis=0)
    tall, wide = density.shape
    col = lax.broadcasted_iota(jnp.int32, (tall, wide), 0) + 248 + lax.axis_index("col") * BC
    row = lax.broadcasted_iota(jnp.int32, (tall, wide), 1)
    row = jnp.where(row < 192, row, row - wide) + lax.axis_index("row") * BR
    inside = (row >= 0) & (row < lax.axis_size("row") * BR) & (col < lax.axis_size("col") * BC)
    inside = jnp.where(inside, 1.0, 0.0)
    density = density * inside
    for _ in range(STEPS):
        beside = (
            pltpu.roll(density, 1, 0)
            + pltpu.roll(density, tall - 1, 0)
            + pltpu.roll(density, 1, 1)
            + pltpu.roll(density, wide - 1, 1)
        )
        density = inside * (0.04 * density + 0.24 * beside)
    share = jnp.concatenate([jnp.zeros((120, 128), F32), density[:8, :128]], axis=0).T
    own[...] = spread[1, :BR] + share
    last = pltpu.make_async_copy(own, density_out.at[:, 128:], sems.at[1])
    last.start()
    first.wait()
    last.wait()


def swap(block, axis, first):
    pairs = range(first, lax.axis_size(axis) - 1, 2)
    return lax.ppermute(block, axis, [p for i in pairs for p in ((i, i + 1), (i + 1, i))])


def shift(block, axis, distance):
    devices = range(lax.axis_size(axis))
    route = [(i, i + distance) for i in devices if i + distance in devices]
    return lax.ppermute(block, axis, route)


def call(kernel, shapes, *args, space=VMEM, outs=None, scratch=()):
    return pl.pallas_call(
        kernel,
        out_shape=[jax.ShapeDtypeStruct(s, F32) for s in shapes],
        in_specs=[pl.BlockSpec(memory_space=space)] * len(args),
        out_specs=[pl.BlockSpec(memory_space=s) for s in outs or [VMEM] * len(shapes)],
        scratch_shapes=list(scratch),
        compiler_params=pltpu.CompilerParams(vmem_limit_bytes=40 * 2**20),
    )(*args)


def body(boxes, pins, cell_bins, cell_area):
    pins = pins.reshape(-1, 128)
    cell_area = cell_area.reshape(-1, 128)
    inputs = (boxes, pins, cell_bins, cell_area)
    inputs = [pltpu.with_memory_space_constraint(a, HBM) for a in inputs]
    d_own, a_own, even, odd = call(
        window_kernel,
        [(BR + 8, WIDE), (BR, BC), (80, WIDE), (80, WIDE)],
        *inputs,
        space=HBM,
        scratch=[pltpu.VMEM(a.shape, a.dtype) for a in inputs]
        + [pltpu.VMEM(pins.shape, F32)] * 2
        + [pltpu.SemaphoreType.DMA((4,))],
    )
    odd = swap(odd, "row", 1)
    even = swap(even, "row", 0)
    d_ext, a_ext, right, left = call(
        merge_kernel,
        [(BR + 16, WIDE), (BR + 16, BC), (BR + 48, 128), (32, 128)],
        d_own,
        a_own,
        odd,
        even,
    )
    left, right = shift(right, "col", 1), shift(left, "col", -1)
    tall = BR + 16
    field = pltpu.VMEM((2, tall, 128), F32)
    two = pltpu.SemaphoreType.DMA((2,))
    spread, mask, over = call(
        middle_kernel,
        [(tall, BC), (tall, BC), (8, 256)],
        d_ext,
        a_ext,
        scratch=[field],
    )
    demand, spread = call(
        low_kernel,
        [(BR, BC), (2, tall, 128)],
        d_ext,
        a_ext,
        spread,
        mask,
        left,
        outs=[HBM, VMEM],
        scratch=[pltpu.VMEM((BR, 128), F32), field, two],
    )
    (density,) = call(
        edge_kernel,
        [(BR, BC)],
        spread,
        over,
        right,
        outs=[HBM],
        scratch=[pltpu.VMEM((BR, 128), F32), two],
    )
    return (demand, density)


def solution(mesh):
    return jax.shard_map(
        body,
        mesh=mesh,
        in_specs=(
            P(None, ("row", "col")),
            P(("row", "col")),
            P(None, ("row", "col")),
            P(("row", "col")),
        ),
        out_specs=(P("row", "col"), P("row", "col")),
        check_vma=False,
    )
```

```python
import jax
import jax.numpy as jnp
from jax import lax
from jax.experimental import pallas as pl
from jax.experimental.pallas import tpu as pltpu
from jax.sharding import PartitionSpec as P

BR = 128
BC = 256
STEPS = 6
PART = (BR + 16) // 8
TALL = 192
WIDE = 384
NET_BLOCK = 2048
CELL_BLOCK = 8192
FACTORS = 24
F32 = jnp.float32
BF16 = jnp.bfloat16
FP8 = jnp.float8_e4m3fn
VMEM = pltpu.MemorySpace.VMEM
HBM = pltpu.MemorySpace.HBM


def repeated(value, rows, dtype):
    if dtype != jnp.int8:
        value = value.astype(F32)
    return jnp.broadcast_to(value, (rows, value.shape[1])).astype(dtype)[None]


def ruler(length, rows, shift, n, dtype):
    shape = (length // rows, rows, n)
    place = lax.broadcasted_iota(jnp.int32, shape, 0) * rows
    place = place + lax.broadcasted_iota(jnp.int32, shape, 1) - shift
    return place.astype(dtype) if dtype == jnp.int8 else place.astype(F32).astype(dtype)


def lane_row(ref, first, n):
    return jnp.concatenate([ref[pl.ds(first // 128 + i, 1), :] for i in range(n // 128)], axis=1)


def nt_dot(left, right):
    return lax.dot_general(left, right, (((1,), (1,)), ((), ())), preferred_element_type=F32)


def split_weights(boxes, pins, row_factor, col_factor):
    width = boxes[3:4, :] - boxes[2:3, :] + 1
    height = boxes[1:2, :] - boxes[0:1, :] + 1
    nets = width.shape[1]
    width, height = (
        jnp.concatenate([v[:, i : i + 128] for i in range(0, nets, 128)], axis=0).astype(F32)
        for v in (width, height)
    )
    weight = pins[...].astype(F32) * (width + height) / (width * height) * (1.0 / 16.0)
    best = weight
    for k in range(FACTORS):
        one = 1.0 + k / 128.0
        other = (weight * (1.0 / one)).astype(BF16).astype(F32)
        error = jnp.abs(other * one - weight)
        if k == 0:
            best, row_part, col_part = error, jnp.ones_like(weight), other
        else:
            better = error < best
            best = jnp.where(better, error, best)
            row_part = jnp.where(better, one, row_part)
            col_part = jnp.where(better, other, col_part)
    row_factor[...] = row_part
    col_factor[...] = col_part


def window_kernel(
    boxes_in, pins_in, bins_in, area_in, d_out, a_out, even_out, odd_out,
    boxes, pins, bins, area, row_factor, col_factor, sems,
):
    half = boxes.shape[1] // 2
    copies = [
        pltpu.make_async_copy(source, target, sems.at[i])
        for i, (source, target) in enumerate(
            (
                (boxes_in.at[:, :half], boxes.at[:, :half]),
                (boxes_in.at[:, half:], boxes.at[:, half:]),
                (pins_in, pins),
                (bins_in, bins),
                (area_in, area),
            )
        )
    ]
    for copy in copies:
        copy.start()
    for copy in copies[:3]:
        copy.wait()
    split_weights(boxes, pins, row_factor, col_factor)
    n = NET_BLOCK
    zero = jnp.zeros((), BF16)

    def add_nets(i, demand):
        k = pl.multiple_of(i * n, n)
        box = boxes[:, pl.ds(k, n)]
        y0, y1, x0, x1 = (box[i : i + 1] for i in range(4))
        top = y0 & (BR - 1)
        bottom = y1 - (y0 - top)
        start = x0 & (BC - 1)
        end = x1 - (x0 - start)
        rows = ruler(TALL, 16, 0, n, BF16)
        inside = (rows >= repeated(top, 16, BF16)) & (rows <= repeated(bottom, 16, BF16))
        down = jnp.where(inside, repeated(lane_row(row_factor, k, n), 16, BF16), zero)
        cols = ruler(WIDE, 16, 192, n, BF16)
        inside = (cols >= repeated(start - 192, 16, BF16)) & (
            cols <= repeated(end - 192, 16, BF16)
        )
        right = jnp.where(inside, repeated(lane_row(col_factor, k, n), 16, BF16), zero)
        return demand + nt_dot(right.reshape(WIDE, n), down.reshape(TALL, n))

    for copy in copies[3:]:
        copy.wait()
    m = CELL_BLOCK
    none = jnp.zeros((), FP8)
    one = jnp.ones((), FP8)

    def add_cells(i, total):
        k = pl.multiple_of(i * m, m)
        where = bins[:, pl.ds(k, m)]
        size = lane_row(area, k, m)
        rows = ruler(BR, 32, 0, m, jnp.int8) == repeated(where[0:1] & (BR - 1), 32, jnp.int8)
        down = jnp.concatenate(
            [
                jnp.where(rows, repeated(part, 32, FP8), none).reshape(BR, m)
                for part in (size >> 3, size & 7)
            ],
            axis=0,
        )
        cols = ruler(BC, 32, 128, m, jnp.int8) == repeated(
            (where[1:2] & (BC - 1)) - 128, 32, jnp.int8
        )
        right = jnp.where(cols, one, none).reshape(BC, m)
        return total + nt_dot(down, right)

    demand, total = lax.fori_loop(
        0,
        boxes.shape[1] // n,
        lambda i, sums: (add_nets(i, sums[0]), add_cells(i, sums[1])),
        (jnp.zeros((WIDE, TALL), F32), jnp.zeros((2 * BR, BC), F32)),
    )
    demand = demand.T
    total = total[:BR] * 0.5 + total[BR:] * (1.0 / 16.0)
    d_out[...] = demand[: BR + 8]
    a_out[...] = total
    even = lax.rem(lax.axis_index("row"), 2) == 0
    for message, goes_down in ((even_out, even), (odd_out, jnp.logical_not(even))):
        message[:8] = jnp.where(goes_down, demand[BR : BR + 8], demand[:8])
        message[8:64] = demand[BR + 8 :]
        message[64:72] = demand[BR - 8 : BR]
        message[72:, :BC] = jnp.where(goes_down, total[BR - 8 :], total[:8])


def lying(strip):
    gap = jnp.zeros((112, 128), F32)
    return jnp.concatenate([strip[: BR + 8], gap, strip[BR + 8 :]], axis=0).T


def merge_kernel(d_own, a_own, odd_in, even_in, d_out, a_out, right_out, left_out):
    even = lax.rem(lax.axis_index("row"), 2) == 0
    above = jnp.where(even, odd_in[...], even_in[...])
    below = jnp.where(even, even_in[:8], odd_in[:8])
    below_area = jnp.where(even, even_in[72:, :BC], odd_in[72:, :BC])
    demand = jnp.concatenate(
        [d_own[:64] + above[:64], d_own[64:BR], d_own[BR:] + below, above[64:72]], axis=0
    )
    area = jnp.concatenate([a_own[...], below_area, above[72:, :BC]], axis=0)
    d_out[...] = demand
    a_out[...] = area
    lane = lax.broadcasted_iota(jnp.int32, (BR + 16, 128), 1)
    first = jnp.where(lane < 8, demand[:, :128], pltpu.roll(area[:, :128], 8, 1))
    strip = jnp.where(lane < 120, pltpu.roll(demand[:, 128:BC], 120, 1), area[:, 128:])
    strip = jnp.where(lane < 16, first, strip)
    strip = lying(strip)
    right_out[: BR + 16] = demand[:, BC:]
    right_out[BR + 16 : BR + 32] = strip[112:, :128]
    right_out[BR + 32 :] = strip[112:, 128:]
    left_out[:16] = strip[:16, :128]
    left_out[16:] = strip[:16, 128:]


def inside_of(col):
    row = lax.broadcasted_iota(jnp.int32, col.shape, 0)
    row = jnp.where(row < BR + 8, row, row - (BR + 16)) + lax.axis_index("row") * BR
    col = col + lax.axis_index("col") * BC
    rows, cols = lax.axis_size("row") * BR, lax.axis_size("col") * BC
    inside = (row >= 0) & (row < rows) & (col >= 0) & (col < cols)
    return jnp.where(inside, 1.0, 0.0)


def inflated(demand, area):
    return (1.0 + 1.5 * demand / (1.0 + demand)) * area


def blocks_of(value, field):
    tiles = range(value.shape[1] // 128)
    for i in tiles:
        field[i] = value[:, 128 * i : 128 * (i + 1)]
    return [
        jnp.concatenate([field[i, pl.ds(k, 8, stride=PART), :] for i in tiles], axis=1)
        for k in range(PART)
    ]


def diffused(block, inner):
    wide = block[0].shape[1]
    for _ in range(STEPS):
        rows = [pltpu.roll(block[-1], 1, 0), *block, pltpu.roll(block[0], 7, 0)]
        block = []
        for k in range(PART):
            mid = rows[k + 1]
            beside = rows[k] + rows[k + 2] + pltpu.roll(mid, 1, 1) + pltpu.roll(mid, wide - 1, 1)
            block.append(inner(k) * (0.04 * mid + 0.24 * beside))
    return block


def upright(strip):
    strip = jnp.concatenate([strip[:16], strip[16:]], axis=1)
    strip = jnp.concatenate([jnp.zeros((112, 256), F32), strip], axis=0).T
    return jnp.concatenate([strip[: BR + 8], strip[248:]], axis=0)


def middle_kernel(d_in, a_in, spread_out, mask_out, over_out, field):
    lane = lax.broadcasted_iota(jnp.int32, (BR + 16, BC), 1)
    for k, block in enumerate(blocks_of(inside_of(jnp.where(lane < 192, lane, lane - BC)), field)):
        mask_out[8 * k : 8 * k + 8] = block
    over_out[...] = lying(d_in[:, BC:])[:8]
    mask = blocks_of(inside_of(jnp.where(lane < 64, lane + BC, lane)), field)
    start = inflated(d_in[:, 128:BC], a_in[:, 128:]) * inside_of(lane[:, 128:])
    start = jnp.concatenate([jnp.zeros((BR + 16, 128), F32), start], axis=1)
    block = diffused(blocks_of(start, field), lambda k: mask[k])
    for k in range(PART):
        spread_out[8 * k : 8 * k + 8] = jnp.where(lane[:8] < 64, 0.0, block[k])


def low_kernel(d_in, a_in, spread, mask, left, demand_out, spread_out, own, field, sems):
    tall = BR + 16
    low = d_in[:, :128] + left[:tall]
    own[...] = low[:BR]
    copies = [
        pltpu.make_async_copy(own, demand_out.at[:, :128], sems.at[0]),
        pltpu.make_async_copy(d_in.at[:BR, 128:BC], demand_out.at[:, 128:], sems.at[1]),
    ]
    for copy in copies:
        copy.start()
    strip = upright(left[tall:])
    lane = lax.broadcasted_iota(jnp.int32, (tall, 128), 1)
    start = jnp.where(lane >= 120, inflated(pltpu.roll(strip, 8, 1), strip), 0.0)
    start = jnp.concatenate([inflated(low, a_in[:, :128]), start], axis=1)
    block = blocks_of(start, field)

    def inner(k):
        return mask[8 * k : 8 * k + 8]

    block = diffused([inner(k) * block[k] for k in range(PART)], inner)
    lane = lax.broadcasted_iota(jnp.int32, (8, BC), 1)
    for k in range(PART):
        known = jnp.where(lane < 192, block[k], 0.0) + spread[8 * k : 8 * k + 8]
        for i in range(2):
            part = known[:, 128 * i : 128 * (i + 1)]
            spread_out[i, pl.ds(k, 8, stride=PART), :] = part
    for copy in copies:
        copy.wait()


def edge_kernel(spread, over, right, density_out, own, sems):
    first = pltpu.make_async_copy(spread.at[0, :BR], density_out.at[:, :128], sems.at[0])
    first.start()
    strip = jnp.concatenate([right[:16], right[16:]], axis=1)
    start = inflated(strip[:8] + over[...], strip[8:])
    none = jnp.zeros((8, 256), F32)
    density = jnp.concatenate([none, start, none], axis=0)
    tall, wide = density.shape
    col = lax.broadcasted_iota(jnp.int32, (tall, wide), 0) + 248 + lax.axis_index("col") * BC
    row = lax.broadcasted_iota(jnp.int32, (tall, wide), 1)
    row = jnp.where(row < 192, row, row - wide) + lax.axis_index("row") * BR
    inside = (row >= 0) & (row < lax.axis_size("row") * BR) & (col < lax.axis_size("col") * BC)
    inside = jnp.where(inside, 1.0, 0.0)
    density = density * inside
    for _ in range(STEPS):
        beside = (
            pltpu.roll(density, 1, 0)
            + pltpu.roll(density, tall - 1, 0)
            + pltpu.roll(density, 1, 1)
            + pltpu.roll(density, wide - 1, 1)
        )
        density = inside * (0.04 * density + 0.24 * beside)
    share = jnp.concatenate([jnp.zeros((120, 128), F32), density[:8, :128]], axis=0).T
    own[...] = spread[1, :BR] + share
    last = pltpu.make_async_copy(own, density_out.at[:, 128:], sems.at[1])
    last.start()
    first.wait()
    last.wait()


def swap(block, axis, first):
    pairs = range(first, lax.axis_size(axis) - 1, 2)
    return lax.ppermute(block, axis, [p for i in pairs for p in ((i, i + 1), (i + 1, i))])


def shift(block, axis, distance):
    devices = range(lax.axis_size(axis))
    route = [(i, i + distance) for i in devices if i + distance in devices]
    return lax.ppermute(block, axis, route)


def call(kernel, shapes, *args, space=VMEM, outs=None, scratch=()):
    return pl.pallas_call(
        kernel,
        out_shape=[jax.ShapeDtypeStruct(s, F32) for s in shapes],
        in_specs=[pl.BlockSpec(memory_space=space)] * len(args),
        out_specs=[pl.BlockSpec(memory_space=s) for s in outs or [VMEM] * len(shapes)],
        scratch_shapes=list(scratch),
        compiler_params=pltpu.CompilerParams(vmem_limit_bytes=40 * 2**20),
    )(*args)


def body(boxes, pins, cell_bins, cell_area):
    pins = pins.reshape(-1, 128)
    cell_area = cell_area.reshape(-1, 128)
    inputs = (boxes, pins, cell_bins, cell_area)
    inputs = [pltpu.with_memory_space_constraint(a, HBM) for a in inputs]
    d_own, a_own, even, odd = call(
        window_kernel,
        [(BR + 8, WIDE), (BR, BC), (80, WIDE), (80, WIDE)],
        *inputs,
        space=HBM,
        scratch=[pltpu.VMEM(a.shape, a.dtype) for a in inputs]
        + [pltpu.VMEM(pins.shape, F32)] * 2
        + [pltpu.SemaphoreType.DMA((5,))],
    )
    odd = swap(odd, "row", 1)
    even = swap(even, "row", 0)
    d_ext, a_ext, right, left = call(
        merge_kernel,
        [(BR + 16, WIDE), (BR + 16, BC), (BR + 48, 128), (32, 128)],
        d_own,
        a_own,
        odd,
        even,
    )
    left, right = shift(right, "col", 1), shift(left, "col", -1)
    tall = BR + 16
    field = pltpu.VMEM((2, tall, 128), F32)
    two = pltpu.SemaphoreType.DMA((2,))
    spread, mask, over = call(
        middle_kernel,
        [(tall, BC), (tall, BC), (8, 256)],
        d_ext,
        a_ext,
        scratch=[field],
    )
    demand, spread = call(
        low_kernel,
        [(BR, BC), (2, tall, 128)],
        d_ext,
        a_ext,
        spread,
        mask,
        left,
        outs=[HBM, VMEM],
        scratch=[pltpu.VMEM((BR, 128), F32), field, two],
    )
    (density,) = call(
        edge_kernel,
        [(BR, BC)],
        spread,
        over,
        right,
        outs=[HBM],
        scratch=[pltpu.VMEM((BR, 128), F32), two],
    )
    return (demand, density)


def solution(mesh):
    return jax.shard_map(
        body,
        mesh=mesh,
        in_specs=(
            P(None, ("row", "col")),
            P(("row", "col")),
            P(None, ("row", "col")),
            P(("row", "col")),
        ),
        out_specs=(P("row", "col"), P("row", "col")),
        check_vma=False,
    )
```

```python
import jax
import jax.numpy as jnp
from jax import lax
from jax.experimental import pallas as pl
from jax.experimental.pallas import tpu as pltpu
from jax.sharding import PartitionSpec as P

BR = 128
BC = 256
STEPS = 6
PART = (BR + 16) // 8
TALL = 192
WIDE = 384
NET_BLOCK = 2048
CELL_BLOCK = 8192
FACTORS = 24
F32 = jnp.float32
BF16 = jnp.bfloat16
FP8 = jnp.float8_e4m3fn
VMEM = pltpu.MemorySpace.VMEM
HBM = pltpu.MemorySpace.HBM


def repeated(value, rows, dtype):
    if dtype != jnp.int8:
        value = value.astype(F32)
    return jnp.broadcast_to(value, (rows, value.shape[1])).astype(dtype)[None]


def ruler(length, rows, shift, n, dtype):
    shape = (length // rows, rows, n)
    place = lax.broadcasted_iota(jnp.int32, shape, 0) * rows
    place = place + lax.broadcasted_iota(jnp.int32, shape, 1) - shift
    return place.astype(dtype) if dtype == jnp.int8 else place.astype(F32).astype(dtype)


def lane_row(ref, first, n):
    return jnp.concatenate([ref[pl.ds(first // 128 + i, 1), :] for i in range(n // 128)], axis=1)


def nt_dot(left, right):
    return lax.dot_general(left, right, (((1,), (1,)), ((), ())), preferred_element_type=F32)


def split_weights(boxes, pins, row_factor, col_factor):
    width = boxes[3:4, :] - boxes[2:3, :] + 1
    height = boxes[1:2, :] - boxes[0:1, :] + 1
    nets = width.shape[1]
    width, height = (
        jnp.concatenate([v[:, i : i + 128] for i in range(0, nets, 128)], axis=0).astype(F32)
        for v in (width, height)
    )
    weight = pins[...].astype(F32) * (width + height) / (width * height) * (1.0 / 16.0)
    best = weight
    for k in range(FACTORS):
        one = 1.0 + k / 128.0
        other = (weight * (1.0 / one)).astype(BF16).astype(F32)
        error = jnp.abs(other * one - weight)
        if k == 0:
            best, row_part, col_part = error, jnp.ones_like(weight), other
        else:
            better = error < best
            best = jnp.where(better, error, best)
            row_part = jnp.where(better, one, row_part)
            col_part = jnp.where(better, other, col_part)
    row_factor[...] = row_part
    col_factor[...] = col_part


def window_kernel(
    boxes_in, pins_in, bins_in, area_in, d_out, a_out, even_out, odd_out,
    boxes, pins, bins, area, row_factor, col_factor, sems,
):
    half = boxes.shape[1] // 2
    copies = [
        pltpu.make_async_copy(source, target, sems.at[i])
        for i, (source, target) in enumerate(
            (
                (boxes_in.at[:, :half], boxes.at[:, :half]),
                (boxes_in.at[:, half:], boxes.at[:, half:]),
                (pins_in, pins),
                (bins_in, bins),
                (area_in, area),
            )
        )
    ]
    for copy in copies:
        copy.start()
    for copy in copies[:3]:
        copy.wait()
    split_weights(boxes, pins, row_factor, col_factor)
    n = NET_BLOCK
    zero = jnp.zeros((), BF16)

    def add_nets(i, demand):
        k = pl.multiple_of(i * n, n)
        box = boxes[:, pl.ds(k, n)]
        y0, y1, x0, x1 = (box[i : i + 1] for i in range(4))
        top = y0 & (BR - 1)
        bottom = y1 - (y0 - top)
        start = x0 & (BC - 1)
        end = x1 - (x0 - start)
        rows = ruler(TALL, 16, 0, n, BF16)
        inside = (rows >= repeated(top, 16, BF16)) & (rows <= repeated(bottom, 16, BF16))
        down = jnp.where(inside, repeated(lane_row(row_factor, k, n), 16, BF16), zero)
        cols = ruler(WIDE, 16, 192, n, BF16)
        inside = (cols >= repeated(start - 192, 16, BF16)) & (
            cols <= repeated(end - 192, 16, BF16)
        )
        right = jnp.where(inside, repeated(lane_row(col_factor, k, n), 16, BF16), zero)
        return demand + nt_dot(right.reshape(WIDE, n), down.reshape(TALL, n))

    for copy in copies[3:]:
        copy.wait()
    m = CELL_BLOCK
    none = jnp.zeros((), FP8)
    one = jnp.ones((), FP8)

    def add_cells(i, total):
        k = pl.multiple_of(i * m, m)
        where = bins[:, pl.ds(k, m)]
        size = lane_row(area, k, m)
        rows = ruler(BR, 32, 0, m, jnp.int8) == repeated(where[0:1] & (BR - 1), 32, jnp.int8)
        down = jnp.concatenate(
            [
                jnp.where(rows, repeated(part, 32, FP8), none).reshape(BR, m)
                for part in (size >> 3, size & 7)
            ],
            axis=0,
        )
        cols = ruler(BC, 32, 128, m, jnp.int8) == repeated(
            (where[1:2] & (BC - 1)) - 128, 32, jnp.int8
        )
        right = jnp.where(cols, one, none).reshape(BC, m)
        return total + nt_dot(down, right)

    total, demand = lax.fori_loop(
        0,
        boxes.shape[1] // n,
        lambda i, sums: (add_cells(i, sums[0]), add_nets(i, sums[1])),
        (jnp.zeros((2 * BR, BC), F32), jnp.zeros((WIDE, TALL), F32)),
    )
    demand = demand.T
    total = total[:BR] * 0.5 + total[BR:] * (1.0 / 16.0)
    d_out[...] = demand[: BR + 8]
    a_out[...] = total
    even = lax.rem(lax.axis_index("row"), 2) == 0
    for message, goes_down in ((even_out, even), (odd_out, jnp.logical_not(even))):
        message[:8] = jnp.where(goes_down, demand[BR : BR + 8], demand[:8])
        message[8:64] = demand[BR + 8 :]
        message[64:72] = demand[BR - 8 : BR]
        message[72:, :BC] = jnp.where(goes_down, total[BR - 8 :], total[:8])


def lying(strip):
    gap = jnp.zeros((112, 128), F32)
    return jnp.concatenate([strip[: BR + 8], gap, strip[BR + 8 :]], axis=0).T


def merge_kernel(d_own, a_own, odd_in, even_in, d_out, a_out, right_out, left_out):
    even = lax.rem(lax.axis_index("row"), 2) == 0
    above = jnp.where(even, odd_in[...], even_in[...])
    below = jnp.where(even, even_in[:8], odd_in[:8])
    below_area = jnp.where(even, even_in[72:, :BC], odd_in[72:, :BC])
    demand = jnp.concatenate(
        [d_own[:64] + above[:64], d_own[64:BR], d_own[BR:] + below, above[64:72]], axis=0
    )
    area = jnp.concatenate([a_own[...], below_area, above[72:, :BC]], axis=0)
    d_out[...] = demand
    a_out[...] = area
    lane = lax.broadcasted_iota(jnp.int32, (BR + 16, 128), 1)
    first = jnp.where(lane < 8, demand[:, :128], pltpu.roll(area[:, :128], 8, 1))
    strip = jnp.where(lane < 120, pltpu.roll(demand[:, 128:BC], 120, 1), area[:, 128:])
    strip = jnp.where(lane < 16, first, strip)
    strip = lying(strip)
    right_out[: BR + 16] = demand[:, BC:]
    right_out[BR + 16 : BR + 32] = strip[112:, :128]
    right_out[BR + 32 :] = strip[112:, 128:]
    left_out[:16] = strip[:16, :128]
    left_out[16:] = strip[:16, 128:]


def inside_of(col):
    row = lax.broadcasted_iota(jnp.int32, col.shape, 0)
    row = jnp.where(row < BR + 8, row, row - (BR + 16)) + lax.axis_index("row") * BR
    col = col + lax.axis_index("col") * BC
    rows, cols = lax.axis_size("row") * BR, lax.axis_size("col") * BC
    inside = (row >= 0) & (row < rows) & (col >= 0) & (col < cols)
    return jnp.where(inside, 1.0, 0.0)


def inflated(demand, area):
    return (1.0 + 1.5 * demand / (1.0 + demand)) * area


def blocks_of(value, field):
    tiles = range(value.shape[1] // 128)
    for i in tiles:
        field[i] = value[:, 128 * i : 128 * (i + 1)]
    return [
        jnp.concatenate([field[i, pl.ds(k, 8, stride=PART), :] for i in tiles], axis=1)
        for k in range(PART)
    ]


def diffused(block, inner):
    wide = block[0].shape[1]
    for _ in range(STEPS):
        rows = [pltpu.roll(block[-1], 1, 0), *block, pltpu.roll(block[0], 7, 0)]
        block = []
        for k in range(PART):
            mid = rows[k + 1]
            beside = rows[k] + rows[k + 2] + pltpu.roll(mid, 1, 1) + pltpu.roll(mid, wide - 1, 1)
            block.append(inner(k) * (0.04 * mid + 0.24 * beside))
    return block


def upright(strip):
    strip = jnp.concatenate([strip[:16], strip[16:]], axis=1)
    strip = jnp.concatenate([jnp.zeros((112, 256), F32), strip], axis=0).T
    return jnp.concatenate([strip[: BR + 8], strip[248:]], axis=0)


def middle_kernel(d_in, a_in, spread_out, mask_out, over_out, field):
    lane = lax.broadcasted_iota(jnp.int32, (BR + 16, BC), 1)
    for k, block in enumerate(blocks_of(inside_of(jnp.where(lane < 192, lane, lane - BC)), field)):
        mask_out[8 * k : 8 * k + 8] = block
    over_out[...] = lying(d_in[:, BC:])[:8]
    mask = blocks_of(inside_of(jnp.where(lane < 64, lane + BC, lane)), field)
    start = inflated(d_in[:, 128:BC], a_in[:, 128:]) * inside_of(lane[:, 128:])
    start = jnp.concatenate([jnp.zeros((BR + 16, 128), F32), start], axis=1)
    block = diffused(blocks_of(start, field), lambda k: mask[k])
    for k in range(PART):
        spread_out[8 * k : 8 * k + 8] = jnp.where(lane[:8] < 64, 0.0, block[k])


def low_kernel(d_in, a_in, spread, mask, left, demand_out, spread_out, own, field, sems):
    tall = BR + 16
    low = d_in[:, :128] + left[:tall]
    own[...] = low[:BR]
    copies = [
        pltpu.make_async_copy(own, demand_out.at[:, :128], sems.at[0]),
        pltpu.make_async_copy(d_in.at[:BR, 128:BC], demand_out.at[:, 128:], sems.at[1]),
    ]
    for copy in copies:
        copy.start()
    strip = upright(left[tall:])
    lane = lax.broadcasted_iota(jnp.int32, (tall, 128), 1)
    start = jnp.where(lane >= 120, inflated(pltpu.roll(strip, 8, 1), strip), 0.0)
    start = jnp.concatenate([inflated(low, a_in[:, :128]), start], axis=1)
    block = blocks_of(start, field)

    def inner(k):
        return mask[8 * k : 8 * k + 8]

    block = diffused([inner(k) * block[k] for k in range(PART)], inner)
    lane = lax.broadcasted_iota(jnp.int32, (8, BC), 1)
    for k in range(PART):
        known = jnp.where(lane < 192, block[k], 0.0) + spread[8 * k : 8 * k + 8]
        for i in range(2):
            part = known[:, 128 * i : 128 * (i + 1)]
            spread_out[i, pl.ds(k, 8, stride=PART), :] = part
    for copy in copies:
        copy.wait()


def edge_kernel(spread, over, right, density_out, own, sems):
    first = pltpu.make_async_copy(spread.at[0, :BR], density_out.at[:, :128], sems.at[0])
    first.start()
    strip = jnp.concatenate([right[:16], right[16:]], axis=1)
    start = inflated(strip[:8] + over[...], strip[8:])
    none = jnp.zeros((8, 256), F32)
    density = jnp.concatenate([none, start, none], axis=0)
    tall, wide = density.shape
    col = lax.broadcasted_iota(jnp.int32, (tall, wide), 0) + 248 + lax.axis_index("col") * BC
    row = lax.broadcasted_iota(jnp.int32, (tall, wide), 1)
    row = jnp.where(row < 192, row, row - wide) + lax.axis_index("row") * BR
    inside = (row >= 0) & (row < lax.axis_size("row") * BR) & (col < lax.axis_size("col") * BC)
    inside = jnp.where(inside, 1.0, 0.0)
    density = density * inside
    for _ in range(STEPS):
        beside = (
            pltpu.roll(density, 1, 0)
            + pltpu.roll(density, tall - 1, 0)
            + pltpu.roll(density, 1, 1)
            + pltpu.roll(density, wide - 1, 1)
        )
        density = inside * (0.04 * density + 0.24 * beside)
    share = jnp.concatenate([jnp.zeros((120, 128), F32), density[:8, :128]], axis=0).T
    own[...] = spread[1, :BR] + share
    last = pltpu.make_async_copy(own, density_out.at[:, 128:], sems.at[1])
    last.start()
    first.wait()
    last.wait()


def swap(block, axis, first):
    pairs = range(first, lax.axis_size(axis) - 1, 2)
    return lax.ppermute(block, axis, [p for i in pairs for p in ((i, i + 1), (i + 1, i))])


def shift(block, axis, distance):
    devices = range(lax.axis_size(axis))
    route = [(i, i + distance) for i in devices if i + distance in devices]
    return lax.ppermute(block, axis, route)


def call(kernel, shapes, *args, space=VMEM, outs=None, scratch=()):
    return pl.pallas_call(
        kernel,
        out_shape=[jax.ShapeDtypeStruct(s, F32) for s in shapes],
        in_specs=[pl.BlockSpec(memory_space=space)] * len(args),
        out_specs=[pl.BlockSpec(memory_space=s) for s in outs or [VMEM] * len(shapes)],
        scratch_shapes=list(scratch),
        compiler_params=pltpu.CompilerParams(vmem_limit_bytes=40 * 2**20),
    )(*args)


def body(boxes, pins, cell_bins, cell_area):
    pins = pins.reshape(-1, 128)
    cell_area = cell_area.reshape(-1, 128)
    inputs = (boxes, pins, cell_bins, cell_area)
    inputs = [pltpu.with_memory_space_constraint(a, HBM) for a in inputs]
    d_own, a_own, even, odd = call(
        window_kernel,
        [(BR + 8, WIDE), (BR, BC), (80, WIDE), (80, WIDE)],
        *inputs,
        space=HBM,
        scratch=[pltpu.VMEM(a.shape, a.dtype) for a in inputs]
        + [pltpu.VMEM(pins.shape, F32)] * 2
        + [pltpu.SemaphoreType.DMA((5,))],
    )
    odd = swap(odd, "row", 1)
    even = swap(even, "row", 0)
    d_ext, a_ext, right, left = call(
        merge_kernel,
        [(BR + 16, WIDE), (BR + 16, BC), (BR + 48, 128), (32, 128)],
        d_own,
        a_own,
        odd,
        even,
    )
    left, right = shift(right, "col", 1), shift(left, "col", -1)
    tall = BR + 16
    field = pltpu.VMEM((2, tall, 128), F32)
    two = pltpu.SemaphoreType.DMA((2,))
    spread, mask, over = call(
        middle_kernel,
        [(tall, BC), (tall, BC), (8, 256)],
        d_ext,
        a_ext,
        scratch=[field],
    )
    demand, spread = call(
        low_kernel,
        [(BR, BC), (2, tall, 128)],
        d_ext,
        a_ext,
        spread,
        mask,
        left,
        outs=[HBM, VMEM],
        scratch=[pltpu.VMEM((BR, 128), F32), field, two],
    )
    (density,) = call(
        edge_kernel,
        [(BR, BC)],
        spread,
        over,
        right,
        outs=[HBM],
        scratch=[pltpu.VMEM((BR, 128), F32), two],
    )
    return (demand, density)


def solution(mesh):
    return jax.shard_map(
        body,
        mesh=mesh,
        in_specs=(
            P(None, ("row", "col")),
            P(("row", "col")),
            P(None, ("row", "col")),
            P(("row", "col")),
        ),
        out_specs=(P("row", "col"), P("row", "col")),
        check_vma=False,
    )
```
